32 devices in a mesh: seq: 8 (over z, x), tp: 4 (over y, core).
Axes of the slice: x: 2, y: 2, z: 4, core: 2. Of those that a mesh axis runs over, the one named last changes fastest.
Arguments:
- tokens: bfloat16 [16384, 768], P('seq'), may hold values from -6 to 6
- cotangent: bfloat16 [16384, 768], P('seq'), may hold values from -6 to 6
- lengths: int32 [256], replicated, may hold values from 1 to 128, 16384 in all
- w_qkv: bfloat16 [3, 768, 768], P(None, None, 'tp'), may hold values from -0.21875 to 0.21875
- qv_bias: float32 [2, 768], P(None, 'tp'), may hold values from -3 to 3
- w_out: bfloat16 [768, 768], P('tp'), may hold values from -0.625 to 0.625
- out_bias: float32 [768], replicated, may hold values from -2 to 2
- gain_first: float32 [768], replicated, may hold values from 0.5 to 1.5
- shift_first: float32 [768], replicated, may hold values from -2 to 2
- w_up: bfloat16 [768, 3072], P(None, 'tp'), may hold values from -0.21875 to 0.21875
- up_bias: float32 [3072], P('tp'), may hold values from -3 to 3
- w_down: bfloat16 [3072, 768], P('tp'), may hold values from -0.15625 to 0.15625
- down_bias: float32 [768], replicated, may hold values from -2 to 2
- gain_second: float32 [768], replicated, may hold values from 0.5 to 1.5
- shift_second: float32 [768], replicated, may hold values from -2 to 2
Outputs:
- activations: bfloat16 [16384, 768], P('seq')
- input_grad: float32 [16384, 768], P('seq')
- grad_qkv: float32 [3, 768, 768], P(None, None, 'tp')
- grad_qv_bias: float32 [2, 768], P(None, 'tp')
- grad_w_out: float32 [768, 768], P('tp')
- grad_out_bias: float32 [768], replicated
- grad_gain_first: float32 [768], replicated
- grad_shift_first: float32 [768], replicated
- grad_w_up: float32 [768, 3072], P(None, 'tp')
- grad_up_bias: float32 [3072], P('tp')
- grad_w_down: float32 [3072, 768], P('tp')
- grad_down_bias: float32 [768], replicated
- grad_gain_second: float32 [768], replicated
- grad_shift_second: float32 [768], replicated
The draws below stay inside these ranges and needn't reach their ends.
Inputs may be any that keep to these rules, and one draw needn't show every extreme that they name: lengths of the 256 sentences in order; they sum to 16384, and the longest is exactly 128.
All inputs are finite; a program needn't handle non-finite values.
Results may differ from the reference program's by a relative error of at most 0.012.
The reference program's roundings to bfloat16 on the way count: a program that leaves them out, or rounds other values in their place, can miss the bound.
Values may be sent and summed in bfloat16 or wider, within the bound.
No kernel may reach another device: no remote copies, remote signals or barrier semaphores. Data moves between devices by JAX's collectives and lax.ppermute only.
A program may use at most 128 MiB of HBM per device.

```python
import math
import jax
import jax.numpy as jnp
import numpy as np
from jax import lax

D = 768
HEADS = 12
HEAD = 64
FF = 3072
MOST = 128
TOKENS = 16384
SENTS = 256


def block_scale(rng, dims, split, smallest, high):
    loudness = 1.0
    for position, blocks in split:
        heights = jax.random.uniform(jax.random.fold_in(jax.random.fold_in(rng, 6), position), (blocks,), jnp.float32, smallest / len(split), high / len(split))
        loudness = loudness * jnp.repeat(jnp.exp(heights), dims[position] // blocks).reshape((-1,) + (1,) * (len(dims) - 1 - position))
    return loudness


def split_up(number_of, total, most, skew):
    portions = [(1 << 20) // math.isqrt(rank ** skew) + 1 for rank in range(2, number_of + 1)]
    surplus, given = total - most - (number_of - 1), [1] * (number_of - 1)
    while surplus > 0:
        candidates = [i for i in range(number_of - 1) if given[i] < most]
        pool, budget = sum([portions[i] for i in candidates]), surplus
        for i in candidates:
            addition = min(most - given[i], max(1, budget * portions[i] // pool), surplus)
            given[i] = given[i] + addition
            surplus = surplus - addition
    return np.array([most] + given)


def ragged(key, number_of, total, most, skew):
    if number_of == 2:
        one = jax.random.randint(key, (), max(1, total - most), min(most, total - 1) + 1)
        return jnp.stack([one, total - one])
    sizes = jnp.asarray(split_up(number_of, total, most, skew), jnp.int32)
    couples = (number_of - 1) // 2
    giver, taker = sizes[1:1 + 2 * couples:2], sizes[2:2 + 2 * couples:2]
    slack = jnp.minimum(giver - 1, most - taker)
    moved = jax.random.randint(jax.random.fold_in(key, 1), (couples,), 0, 1 << 20) % (slack + 1)
    sizes = sizes.at[1:1 + 2 * couples:2].set(giver - moved).at[2:2 + 2 * couples:2].set(taker + moved)
    return sizes[jax.random.permutation(jax.random.fold_in(key, 2), number_of)]


def scatter_about(rng, dims, spread, bound, shards=(), held_as=jnp.bfloat16):
    values = jax.random.normal(rng, dims, jnp.float32) * spread
    if len(shards) > 0:
        values = block_scale(rng, dims, shards, -0.22, 0.18) * values
    return jnp.clip(values, min=-bound, max=bound).astype(held_as)


def setup_inputs(seed: int = 0) -> dict:
    streams_of = jax.random.split(jax.random.key(seed), 16)
    tokens = scatter_about(streams_of[0], (TOKENS, D), 1.0, 6.0, ((0, 8),))
    cotangent = scatter_about(streams_of[1], (TOKENS, D), 1.0, 6.0, ((0, 8),))
    lengths = ragged(streams_of[2], SENTS, TOKENS, MOST, 1).astype(jnp.int32)
    w_qkv = scatter_about(streams_of[3], (3, D, D), D ** -0.5, 0.21875, ((2, 4),))
    qv_bias = scatter_about(streams_of[4], (2, D), 0.5, 3.0, ((1, 4),), jnp.float32)
    w_out = scatter_about(streams_of[5], (D, D), (D // 8) ** -0.5, 0.625, ((0, 4),))
    out_bias = scatter_about(streams_of[6], (D,), 0.3, 2.0, (), jnp.float32)
    gain_first = jnp.clip(1.0 + 0.1 * jax.random.normal(streams_of[7], (D,), jnp.float32), 0.5, 1.5)
    shift_first = scatter_about(streams_of[8], (D,), 0.3, 2.0, (), jnp.float32)
    w_up = scatter_about(streams_of[9], (D, FF), D ** -0.5, 0.21875, ((1, 4),))
    up_bias = scatter_about(streams_of[10], (FF,), 0.5, 3.0, ((0, 4),), jnp.float32)
    w_down = scatter_about(streams_of[11], (FF, D), (FF // 2) ** -0.5, 0.15625, ((0, 4),))
    down_bias = scatter_about(streams_of[12], (D,), 0.3, 2.0, (), jnp.float32)
    gain_second = jnp.clip(1.0 + 0.1 * jax.random.normal(streams_of[13], (D,), jnp.float32), 0.5, 1.5)
    shift_second = scatter_about(streams_of[14], (D,), 0.3, 2.0, (), jnp.float32)
    return {"tokens": tokens, "cotangent": cotangent, "lengths": lengths, "w_qkv": w_qkv, "qv_bias": qv_bias, "w_out": w_out, "out_bias": out_bias, "gain_first": gain_first, "shift_first": shift_first, "w_up": w_up, "up_bias": up_bias, "w_down": w_down, "down_bias": down_bias, "gain_second": gain_second, "shift_second": shift_second}


EPS = 1e-12

@jax.custom_vjp
def low(v):
    return lax.optimization_barrier(v.astype(jnp.bfloat16)).astype(jnp.float32)

@jax.custom_vjp
def low_back(v):
    return v

def low_keep(v):
    return (low(v), None)

def low_pass(kept, grad):
    return (grad,)

def back_keep(v):
    return (v, None)

def back_low(kept, grad):
    return (low(grad),)
low.defvjp(low_keep, low_pass)
low_back.defvjp(back_keep, back_low)

def matmul(left, right):
    return jnp.dot(left, right, precision=lax.Precision.HIGHEST, preferred_element_type=jnp.float32)

def norm_rows(resid, scale_row, shift_row):
    row_mean = lax.optimization_barrier(jnp.mean(resid, -1, keepdims=True))
    centred = resid - row_mean
    variance = lax.optimization_barrier(jnp.mean(centred * centred, -1, keepdims=True))
    return centred * lax.rsqrt(variance + EPS) * scale_row + shift_row

def sentence_ids(lengths, places, all_rows):
    sent_ends = jnp.cumsum(lengths).astype(jnp.int32)
    passed = lax.optimization_barrier(jnp.sum((sent_ends[None, :] <= places[:, None]).astype(jnp.int32), 1))
    return jnp.where((places < 0) | (places >= all_rows), -1, passed).astype(jnp.int32)

def forward(inputs_f, w_qkv, qv_bias, w_out, out_bias, gain_first, shift_first, w_up, up_bias, w_down, down_bias, gain_second, shift_second, sent_of):
    inputs = low(inputs_f)
    queries = low(low_back(matmul(inputs, w_qkv[0]) + qv_bias[0]))
    keys_all = low(low_back(matmul(inputs, w_qkv[1])))
    values_all = low(low_back(matmul(inputs, w_qkv[2]) + qv_bias[1]))
    block_rows = min(512, TOKENS)
    window = block_rows + 2 * MOST
    keys_pad = jnp.pad(keys_all, ((MOST, MOST), (0, 0)))
    values_pad = jnp.pad(values_all, ((MOST, MOST), (0, 0)))
    sent_pad = jnp.pad(sent_of, (MOST, MOST), constant_values=-1)

    def attend(first_row):
        query_blk = lax.dynamic_slice_in_dim(queries, first_row, block_rows, 0).reshape(block_rows, HEADS, HEAD)
        key_blk = lax.dynamic_slice_in_dim(keys_pad, first_row, window, 0).reshape(window, HEADS, HEAD)
        value_blk = lax.dynamic_slice_in_dim(values_pad, first_row, window, 0).reshape(window, HEADS, HEAD)
        query_sent = lax.dynamic_slice_in_dim(sent_of, first_row, block_rows, 0)
        key_sent = lax.dynamic_slice_in_dim(sent_pad, first_row, window, 0)
        scores = low_back(jnp.einsum('qhd,khd->hqk', query_blk, key_blk, precision=lax.Precision.HIGHEST) * HEAD ** (-0.5))
        scores = jnp.where((query_sent[:, None] == key_sent[None, :])[None], scores, -1e+30)
        row_max = lax.optimization_barrier(jnp.max(scores, -1, keepdims=True))
        raised = jnp.exp(scores - row_max)
        weights = low(raised / lax.optimization_barrier(jnp.sum(raised, -1, keepdims=True)))
        mixed_blk = jnp.einsum('hqk,khd->qhd', weights, value_blk, precision=lax.Precision.HIGHEST)
        return mixed_blk.reshape(block_rows, D)
    starts = jnp.arange(TOKENS // block_rows, dtype=jnp.int32) * block_rows
    mixed = lax.map(jax.checkpoint(attend), starts).reshape(TOKENS, D)
    mixed = low(low_back(mixed))
    attn = low_back(matmul(mixed, w_out) + out_bias)
    first_out = norm_rows(inputs_f + attn, gain_first, shift_first)
    first_low = low(first_out)
    upward = low_back(matmul(first_low, w_up) + up_bias)
    activated = low(jax.nn.gelu(upward, approximate=False))
    downward = low_back(matmul(activated, w_down) + down_bias)
    return norm_rows(first_out + downward, gain_second, shift_second)

def reference(tokens, cotangent, lengths, w_qkv, qv_bias, w_out, out_bias, gain_first, shift_first, w_up, up_bias, w_down, down_bias, gain_second, shift_second):
    sent_of = sentence_ids(lengths, jnp.arange(TOKENS, dtype=jnp.int32), TOKENS)
    params = [arr.astype(jnp.float32) for arr in (tokens, w_qkv, qv_bias, w_out, out_bias, gain_first, shift_first, w_up, up_bias, w_down, down_bias, gain_second, shift_second)]

    def layer(*values):
        return forward(*values, sent_of)
    result, pullback = jax.vjp(layer, *params)
    grads = pullback(cotangent.astype(jnp.float32))
    return (result.astype(jnp.bfloat16), grads[0], grads[1], grads[2], grads[3], grads[4], grads[5], grads[6], grads[7], grads[8], grads[9], grads[10], grads[11], grads[12])
```

```python
import jax
import jax.numpy as jnp
from jax import lax
from jax.experimental import pallas as pl
from jax.experimental.pallas import tpu as pltpu
from jax.sharding import PartitionSpec as P

HEAD = 64
MOST = 128
EPS = 1e-12
BF = jnp.bfloat16
F32 = jnp.float32
MIB = 1024 * 1024


def nn(left, right):
    return lax.dot_general(left, right, (((1,), (0,)), ((), ())), preferred_element_type=F32)


def nt(left, right):
    return lax.dot_general(left, right, (((1,), (1,)), ((), ())), preferred_element_type=F32)


def tn(left, right):
    return lax.dot_general(left, right, (((0,), (0,)), ((), ())), preferred_element_type=F32)


VMEM = pl.BlockSpec(memory_space=pltpu.VMEM)
SMEM = pl.BlockSpec(memory_space=pltpu.SMEM)


ANY = pl.BlockSpec(memory_space=pl.ANY)


def call(body, outs, specs, name, args, after=(), scratch=(), limit=56):
    given = len(args)

    def whole(*refs):
        body(*refs[:given], *refs[given + len(after) :])

    return pl.pallas_call(
        whole,
        out_shape=[jax.ShapeDtypeStruct(shape, dtype) for shape, dtype in outs],
        in_specs=list(specs) + [ANY] * len(after),
        out_specs=[VMEM] * len(outs),
        scratch_shapes=list(scratch),
        name=name,
        cost_estimate=pl.CostEstimate(flops=0, bytes_accessed=0, transcendentals=0),
        compiler_params=pltpu.CompilerParams(vmem_limit_bytes=limit * MIB),
    )(*args, *after)


def stack_heads(block, heads):
    lane = lax.broadcasted_iota(jnp.int32, block.shape, 1) // HEAD
    zero = jnp.zeros_like(block)
    return jnp.concatenate([jnp.where(lane == h, block, zero) for h in range(heads)], 0)


def pick_heads(stacked, heads):
    rows = stacked.shape[0] // heads
    lane = lax.broadcasted_iota(jnp.int32, (rows, stacked.shape[1]), 1) // HEAD
    out = stacked[:rows]
    for h in range(1, heads):
        out = jnp.where(lane == h, stacked[h * rows : (h + 1) * rows], out)
    return out


def attend_body(
    place, tokens, low, high, wt, bias, ids_col, ids_row, q_out, k_out, v_out, p_out, mixed_out
):
    rows = tokens.shape[0]
    cols = wt.shape[1]
    heads = cols // HEAD
    quarter = mixed_out.shape[1]
    scale = jnp.asarray(HEAD**-0.5, BF)

    def project(source, first, size, target, with_q):
        block = source[pl.ds(first, size), :]
        k_out[pl.ds(target, size), :] = nt(block, wt[1]).astype(BF)
        v_out[pl.ds(target, size), :] = (nt(block, wt[2]) + bias[1:2, :]).astype(BF)
        if with_q:
            q_out[pl.ds(first, size), :] = (nt(block, wt[0]) + bias[0:1, :]).astype(BF)

    project(low, 0, MOST, 0, False)
    project(high, 0, MOST, rows + MOST, False)
    step = 256

    @pl.loop(0, rows // step)
    def _(i):
        first = pl.multiple_of(i * step, step)
        project(tokens, first, step, pl.multiple_of(first + MOST, MOST), True)

    @pl.loop(0, rows // MOST)
    def _(b):
        first = pl.multiple_of(b * MOST, MOST)
        q3 = stack_heads(q_out[pl.ds(first, MOST), :] * scale, heads)
        scores = nt(q3, k_out[pl.ds(first, 3 * MOST), :])
        mine = ids_col[pl.ds(pl.multiple_of(first + MOST, MOST), MOST), :]
        mask = mine == ids_row[:, pl.ds(first, 3 * MOST)]
        scores = jnp.where(jnp.concatenate([mask] * heads, 0), scores, -1e30)
        raised = jnp.exp(scores - jnp.max(scores, -1, keepdims=True))
        probs = raised * (1.0 / jnp.sum(raised, -1, keepdims=True))
        probs = probs.astype(BF)
        p_out[b] = probs
        mixed = pick_heads(nn(probs, v_out[pl.ds(first, 3 * MOST), :]), heads)
        per = quarter // MOST
        mixed_out[(b // per) ^ place[0], pl.ds(pl.multiple_of((b % per) * MOST, MOST), MOST), :] = (
            mixed.astype(BF)
        )


def attend(place, tokens, low, high, wt, bias, ids_col, ids_row, after=()):
    rows, cols = tokens.shape[0], wt.shape[1]
    heads = cols // HEAD
    ext = rows + 2 * MOST
    return call(
        attend_body,
        [
            ((rows, cols), BF),
            ((ext, cols), BF),
            ((ext, cols), BF),
            ((rows // MOST, heads * MOST, 3 * MOST), BF),
            ((4, rows // 4, cols), BF),
        ],
        [SMEM] + [VMEM] * 7,
        "attend",
        (place, tokens, low, high, wt, bias, ids_col, ids_row),
        after,
    )


def attend_back_body(place, q, k, v, probs, g0, g1, g2, g3, dq_out, dk_out, dv_out, grads):
    rows, cols = q.shape
    heads = cols // HEAD
    quarter = g0.shape[0]
    scale = jnp.asarray(HEAD**-0.5, BF)
    for rel, ref in enumerate((g0, g1, g2, g3)):
        grads[pl.ds(pl.multiple_of((place[0] ^ rel) * quarter, quarter), quarter), :] = ref[...]
    dk_out[...] = jnp.zeros_like(dk_out)
    dv_out[...] = jnp.zeros_like(dv_out)

    @pl.loop(0, rows // MOST)
    def _(b):
        first = pl.multiple_of(b * MOST, MOST)
        span = pl.ds(first, 3 * MOST)
        g_stack = stack_heads(grads[pl.ds(first, MOST), :], heads)
        q_stack = stack_heads(q[pl.ds(first, MOST), :] * scale, heads)
        p_low = probs[b]
        weights = p_low.astype(F32)
        grad_probs = nt(g_stack, v[span, :])
        inner = jnp.sum(weights * grad_probs, -1, keepdims=True)
        grad_scores = (weights * (grad_probs - inner)).astype(BF)
        dv_out[span, :] += tn(p_low, g_stack)
        dk_out[span, :] += tn(grad_scores, q_stack)
        dq = pick_heads(nn(grad_scores, k[span, :]), heads) * (HEAD**-0.5)
        dq_out[pl.ds(first, MOST), :] = dq.astype(BF)


def attend_back(place, q, k, v, probs, grads, after=()):
    rows, cols = q.shape
    ext = rows + 2 * MOST
    return call(
        attend_back_body,
        [((rows, cols), BF), ((ext, cols), F32), ((ext, cols), F32)],
        [SMEM] + [VMEM] * 8,
        "attend_back",
        (place, q, k, v, probs, *grads),
        after,
        scratch=[pltpu.VMEM((rows, cols), BF)],
    )


def project_back_body(place, tokens, dq, dk, dv, wt, dwt_out, keep_out, send_out):
    rows = tokens.shape[0]
    quarter = rows // 4
    for j, ref in enumerate((dq, dk, dv)):
        dwt_out[j] = tn(ref[...], tokens[...])
    for rel in range(4):
        here = pl.ds(pl.multiple_of((place[0] ^ rel) * quarter, quarter), quarter)
        part = nn(dq[here, :], wt[0]) + nn(dk[here, :], wt[1]) + nn(dv[here, :], wt[2])
        if rel % 2 == 0:
            keep_out[rel // 2] = part
        else:
            send_out[rel // 2] = part.astype(BF)


def project_back(place, tokens, dq, dk, dv, wt, after=()):
    rows, width = tokens.shape
    cols = wt.shape[1]
    return call(
        project_back_body,
        [
            ((3, cols, width), F32),
            ((2, rows // 4, width), F32),
            ((2, rows // 4, width), BF),
        ],
        [SMEM] + [VMEM] * 5,
        "project_back",
        (place, tokens, dq, dk, dv, wt),
        after,
    )


def gelu_parts(pre):
    size = jnp.abs(pre) * (0.5**0.5)
    bell = jnp.exp(-size * size)
    t = 1.0 / (1.0 + 0.3275911 * size)
    poly = 1.061405429
    for c in (-1.453152027, 1.421413741, -0.284496736, 0.254829592):
        poly = poly * t + c
    tail = 0.5 * poly * t * bell
    cdf = jnp.where(pre >= 0, 1.0 - tail, tail)
    return pre * cdf, cdf + pre * bell * 0.3989422804014327


def norm_stats(resid):
    centred = resid - jnp.mean(resid, -1, keepdims=True)
    inv = lax.rsqrt(jnp.mean(centred * centred, -1, keepdims=True) + EPS)
    return centred * inv, inv


def norm_pull(grad, normed, inv, gain):
    scaled = grad * gain
    return inv * (
        scaled
        - jnp.mean(scaled, -1, keepdims=True)
        - normed * jnp.mean(scaled * normed, -1, keepdims=True)
    )


def col_sum(values):
    return jnp.sum(values, 0, keepdims=True)


STEP = 256
OUT_BIAS, GAIN1, SHIFT1, DOWN_BIAS, GAIN2, SHIFT2 = range(6)


def forward_body(
    tokens, m0, m1, m2, m3, o0, o1, o2, o3, u0, u1, u2, u3, up_bias, rows_in,
    normed_out, inv_out, low_out, act_out, slope_out, first,
):
    attn = rows_in[OUT_BIAS : OUT_BIAS + 1, :]
    for m, o in ((m0, o0), (m1, o1), (m2, o2), (m3, o3)):
        attn = attn + nn(m[...], o[...])
    normed, inv = norm_stats(tokens[...].astype(F32) + attn)
    normed_out[...] = normed
    inv_out[...] = inv
    first[...] = (normed * rows_in[GAIN1 : GAIN1 + 1, :] + rows_in[SHIFT1 : SHIFT1 + 1, :]).astype(BF)
    low_out[...] = first[...]
    for rel, u in enumerate((u0, u1, u2, u3)):

        @pl.loop(0, u.shape[1] // STEP)
        def _(j):
            here = pl.ds(pl.multiple_of(j * STEP, STEP), STEP)
            pre = nn(first[...], u[:, here]) + up_bias[rel : rel + 1, here]
            act, slope = gelu_parts(pre)
            act_out[rel, :, here] = act.astype(BF)
            slope_out[rel, :, here] = slope


def forward(tokens, mixed, outs, ups, up_bias, rows_in, after=()):
    rows, width = tokens.shape
    hidden = ups[0].shape[1]
    return call(
        forward_body,
        [
            ((rows, width), F32),
            ((rows, 1), F32),
            ((rows, width), BF),
            ((4, rows, hidden), BF),
            ((4, rows, hidden), F32),
        ],
        [VMEM] * 15,
        "forward",
        (tokens, *mixed, *outs, *ups, up_bias, rows_in),
        after,
        scratch=[pltpu.VMEM((rows, width), BF)],
    )


def middle_body(
    normed1, act, w0, w1, w2, w3, cot, rows_in,
    result_out, res2_out, low_out, keep_out, send_out, sums_out,
):
    first = normed1[...] * rows_in[GAIN1 : GAIN1 + 1, :] + rows_in[SHIFT1 : SHIFT1 + 1, :]
    down = rows_in[DOWN_BIAS : DOWN_BIAS + 1, :]
    for rel, w in enumerate((w0, w1, w2, w3)):
        down = down + nn(act[rel], w[...])
    gain2 = rows_in[GAIN2 : GAIN2 + 1, :]
    normed, inv = norm_stats(first + down)
    result_out[...] = (normed * gain2 + rows_in[SHIFT2 : SHIFT2 + 1, :]).astype(BF)
    grad = cot[...].astype(F32)
    res2 = norm_pull(grad, normed, inv, gain2)
    res2_out[...] = res2
    low = res2.astype(BF)
    low_out[...] = low
    sums_out[0:1, :] = col_sum(grad * normed)
    sums_out[1:2, :] = col_sum(grad)
    sums_out[2:3, :] = col_sum(low.astype(F32))
    for rel in range(4):
        out = send_out if rel % 2 else keep_out
        out[rel // 2] = tn(act[rel], low_out[...]).astype(BF)


def middle(normed1, act, downs, cot, rows_in, after=()):
    rows, width = normed1.shape
    hidden = act.shape[2]
    return call(
        middle_body,
        [
            ((rows, width), BF),
            ((rows, width), F32),
            ((rows, width), BF),
            ((2, hidden, width), BF),
            ((2, hidden, width), BF),
            ((3, width), F32),
        ],
        [VMEM] * 8,
        "middle",
        (normed1, act, *downs, cot, rows_in),
        after,
    )


def backward_body(
    low2, res2, normed1, inv1, slope, w0, w1, w2, w3, u0, u1, u2, u3, o0, o1, o2, o3, rows_in,
    gup_out, res1_out, low_out, gm_out, sums_out, ups_out, total,
):
    total[...] = res2[...]
    for rel, (w, u) in enumerate(((w0, u0), (w1, u1), (w2, u2), (w3, u3))):

        @pl.loop(0, u.shape[1] // STEP)
        def _(j):
            here = pl.ds(pl.multiple_of(j * STEP, STEP), STEP)
            grad_act = nt(low2[...], w[here, :])
            low = (grad_act * slope[rel, :, here]).astype(BF)
            gup_out[rel, :, here] = low
            ups_out[rel : rel + 1, here] = col_sum(low.astype(F32))

        total[...] += nt(gup_out[rel], u[...])
    grad = total[...]
    res1 = norm_pull(grad, normed1[...], inv1[...], rows_in[GAIN1 : GAIN1 + 1, :])
    res1_out[...] = res1
    low = res1.astype(BF)
    low_out[...] = low
    sums_out[0:1, :] = col_sum(grad * normed1[...])
    sums_out[1:2, :] = col_sum(grad)
    sums_out[2:3, :] = col_sum(low.astype(F32))
    for rel, o in enumerate((o0, o1, o2, o3)):
        gm_out[rel] = nt(low, o[...]).astype(BF)


def backward(low2, res2, normed1, inv1, slope, downs, ups, outs, rows_in, after=()):
    rows, width = low2.shape
    hidden = slope.shape[2]
    cols = outs[0].shape[0]
    return call(
        backward_body,
        [
            ((4, rows, hidden), BF),
            ((rows, width), F32),
            ((rows, width), BF),
            ((4, rows, cols), BF),
            ((3, width), F32),
            ((4, hidden), F32),
        ],
        [VMEM] * 18,
        "backward",
        (low2, res2, normed1, inv1, slope, *downs, *ups, *outs, rows_in),
        after,
        scratch=[pltpu.VMEM((rows, width), F32)],
    )


def weight_grads_body(low1, gup, grad_low, m0, m1, m2, m3, keep_out, send_out):
    cols = m0.shape[1]
    for rel, m in enumerate((m0, m1, m2, m3)):
        out = send_out if rel % 2 else keep_out
        out[rel // 2, 0:cols, :] = tn(m[...], grad_low[...]).astype(BF)
        out[rel // 2, cols:, :] = tn(low1[...], gup[rel]).astype(BF)


def weight_grads(low1, gup, grad_low, mixed, after=()):
    width, hidden = low1.shape[1], gup.shape[2]
    cols = mixed[0].shape[1]
    return call(
        weight_grads_body,
        [((2, cols + width, hidden), BF), ((2, cols + width, hidden), BF)],
        [VMEM] * 7,
        "weight_grads",
        (low1, gup, grad_low, *mixed),
        after,
    )


def place_rows_body(place, p0, p1, p2, p3, out):
    quarter = p0.shape[0]
    for rel, p in enumerate((p0, p1, p2, p3)):
        here = pl.ds(pl.multiple_of((place[0] ^ rel) * quarter, quarter), quarter)
        out[here, :] = p[...].astype(out.dtype)


def place_rows(place, parts, dtype):
    quarter, width = parts[0].shape
    return call(
        place_rows_body,
        [((4 * quarter, width), dtype)],
        [SMEM] + [VMEM] * 4,
        "place_rows",
        (place, *parts),
    )[0]


def swap(value, axis, bits):
    count = lax.axis_size(axis)
    return lax.ppermute(value, axis, [(i, i ^ bits) for i in range(count)])


def gather_rel(own):
    far = swap(own, "tp", 2)
    return (own, swap(own, "tp", 1), far, swap(far, "tp", 1))


def core_sum(keep, send):
    two = keep.astype(F32) + swap(send, "tp", 1).astype(F32)
    return two[0], two[1].astype(BF)


def chip_sum(pair):
    return pair[0] + swap(pair[1], "tp", 2).astype(F32)


def sum_over_seq(part):
    count = lax.axis_size("seq")
    place = lax.axis_index("seq")
    bits = [1 << k for k in range(count.bit_length() - 1)]
    halved = bits[:3]
    for bit in halved:
        half = part.shape[0] // 2
        upper = (place & bit) != 0
        low, high = part[:half], part[half:]
        send = jnp.where(upper, low, high).astype(BF)
        keep = jnp.where(upper, high, low)
        part = keep + swap(send, "seq", bit).astype(F32)
    for bit in bits[3:]:
        mine = part.astype(BF)
        part = mine.astype(F32) + swap(mine, "seq", bit).astype(F32)
    part = part.astype(BF)
    for bit in halved[::-1]:
        other = swap(part, "seq", bit)
        upper = (place & bit) != 0
        part = jnp.concatenate(
            [jnp.where(upper, other, part), jnp.where(upper, part, other)], 0
        )
    return part.astype(F32)


def on_device(
    tokens, cotangent, lengths, w_qkv, qv_bias, w_out, out_bias, gain_first, shift_first,
    w_up, up_bias, w_down, down_bias, gain_second, shift_second,
):
    rows, width = tokens.shape
    quarter = rows // 4
    cols = w_qkv.shape[2]
    hidden = w_up.shape[1]
    seq_count = lax.axis_size("seq")
    tp_place = lax.axis_index("tp")
    seq_place = lax.axis_index("seq")
    place = tp_place.astype(jnp.int32).reshape(1)
    forwards = [(i, i + 1) for i in range(seq_count - 1)]
    backwards = [(b, a) for a, b in forwards]

    low = lax.ppermute(tokens[rows - MOST :], "seq", forwards)
    high = lax.ppermute(tokens[:MOST], "seq", backwards)
    outs = gather_rel(w_out)
    ups = gather_rel(w_up)
    downs = gather_rel(w_down)
    own_bias = up_bias.reshape(1, -1)
    chip_bias = jnp.concatenate([own_bias, swap(own_bias, "tp", 1)], 0)
    up_rows = jnp.concatenate([chip_bias, swap(chip_bias, "tp", 2)], 0)
    zero = jnp.zeros_like(out_bias)
    rows_in = jnp.stack(
        [out_bias, gain_first, shift_first, down_bias, gain_second, shift_second, zero, zero]
    )

    places = seq_place * rows + jnp.arange(rows + 2 * MOST, dtype=jnp.int32) - MOST
    ends = jnp.cumsum(lengths)
    passed = jnp.sum((ends[None, :] <= places[:, None]).astype(jnp.int32), 1)
    ids = jnp.where((places < 0) | (places >= rows * seq_count), -1, passed)

    wt = jnp.transpose(w_qkv, (0, 2, 1))
    q, k, v, probs, mixed = attend(
        place, tokens, low, high, wt, qv_bias, ids[:, None], ids[None, :]
    )
    mixed = [mixed[0]] + [swap(mixed[r], "tp", r) for r in (1, 2, 3)]

    here = tp_place * quarter
    tokens_here = lax.dynamic_slice_in_dim(tokens, here, quarter, 0)
    cot_here = lax.dynamic_slice_in_dim(cotangent, here, quarter, 0)
    normed1, inv1, low1, act, slope = forward(tokens_here, mixed, outs, ups, up_rows, rows_in)
    result, res2, low2, keep_d, send_d, sums2 = middle(normed1, act, downs, cot_here, rows_in)
    result = gather_rel(result)
    pair_d = core_sum(keep_d, send_d)
    gup, res1, grad_low, gm, sums1, up_sums = backward(
        low2, res2, normed1, inv1, slope, downs, ups, outs, rows_in
    )
    gm = [gm[0]] + [swap(gm[r], "tp", r) for r in (1, 2, 3)]
    keep_u, send_u = weight_grads(low1, gup, grad_low, mixed, pair_d)
    pair_u = core_sum(keep_u, send_u)
    dq, dk, dv = attend_back(place, q, k, v, probs, gm, pair_u)
    part_d = chip_sum(pair_d)

    pair = jnp.stack([dk, dv])
    to_low = lax.ppermute(pair[:, :MOST].astype(BF), "seq", backwards).astype(F32)
    to_high = lax.ppermute(pair[:, rows + MOST :].astype(BF), "seq", forwards).astype(F32)
    own = pair[:, MOST : rows + MOST]
    own = jnp.concatenate(
        [own[:, :MOST] + to_high, own[:, MOST : rows - MOST], own[:, rows - MOST :] + to_low], 1
    ).astype(BF)
    dk, dv = own[0], own[1]
    dwt, keep_i, send_i = project_back(place, tokens, dq, dk, dv, wt, (part_d,))
    grad_qkv = sum_over_seq(dwt.reshape(3 * cols, width)).reshape(3, cols, width)
    grad_qkv = jnp.transpose(grad_qkv, (0, 2, 1))
    grad_down = sum_over_seq(part_d)
    grad_bundle = sum_over_seq(chip_sum(pair_u))
    input_part = lax.optimization_barrier((chip_sum(core_sum(keep_i, send_i)) + res1).astype(BF))
    input_grad = place_rows(place, gather_rel(input_part), F32)
    result = place_rows(place, result, BF)

    sums = jnp.concatenate([sums2, sums1], 0)
    other = swap(jnp.concatenate([sums, up_sums[1::2]], 0), "tp", 1)
    sums, up_sums = sums + other[:6], up_sums[0::2] + other[6:]
    other = swap(jnp.concatenate([sums, up_sums[1:]], 0), "tp", 2)
    sums, up_sums = sums + other[:6], up_sums[:1] + other[6:]
    qv_sums = jnp.stack([jnp.sum(dq.astype(F32), 0), jnp.sum(dv.astype(F32), 0)])
    qv_row = jnp.pad(qv_sums.reshape(1, -1), ((0, 0), (0, width - 2 * cols)))
    sums = jnp.concatenate([sums, up_sums, qv_row], 0)
    for k in range(seq_count.bit_length() - 1):
        sums = sums + swap(sums, "seq", 1 << k)
    qv_sums = sums[7, : 2 * cols].reshape(2, cols)
    return (
        result, input_grad, grad_qkv, qv_sums, grad_bundle[:cols], sums[5], sums[3], sums[4],
        grad_bundle[cols:], sums[6], grad_down, sums[2], sums[0], sums[1],
    )


def solution(mesh):
    rep, rows = P(), P("seq", None)
    return jax.shard_map(
        on_device,
        mesh=mesh,
        in_specs=(
            rows, rows, rep, P(None, None, "tp"), P(None, "tp"), P("tp", None), rep, rep, rep,
            P(None, "tp"), P("tp"), P("tp", None), rep, rep, rep,
        ),
        out_specs=(
            rows, rows, P(None, None, "tp"), P(None, "tp"), P("tp", None), rep, rep, rep,
            P(None, "tp"), P("tp"), P("tp", None), rep, rep, rep,
        ),
        check_vma=False,
    )
```

```python
import functools
import types

import jax
import jax.numpy as jnp
from jax import lax
from jax.experimental import pallas as pl
from jax.experimental.pallas import tpu as pltpu
from jax.sharding import PartitionSpec as P

HEAD = 64
MOST = 128
EPS = 1e-12
BF = jnp.bfloat16
F32 = jnp.float32
MIB = 1024 * 1024


def nn(left, right):
    return lax.dot_general(left, right, (((1,), (0,)), ((), ())), preferred_element_type=F32)


def nt(left, right):
    return lax.dot_general(left, right, (((1,), (1,)), ((), ())), preferred_element_type=F32)


def tn(left, right):
    return lax.dot_general(left, right, (((0,), (0,)), ((), ())), preferred_element_type=F32)


VMEM = pl.BlockSpec(memory_space=pltpu.VMEM)
SMEM = pl.BlockSpec(memory_space=pltpu.SMEM)


COST = {
    "prepare": 2, "project": 3, "attend": 5, "forward": 6, "middle": 5, "backward": 6, "up_grads": 0.5, "out_grads": 0.5,
    "attend_back": 4, "rims": 4, "input_back": 3, "qkv_grads": 12, "place_rows": 2,
}
ANY = pl.BlockSpec(memory_space=pl.ANY)


def call(
    body, outs, specs, name, args, after=(), through=(), scratch=(), limit=56, lazy=(), late=(), parts=None
):
    given, extra, made = len(args), len(after) + len(through), len(outs)
    rows_of = dict(lazy) if isinstance(lazy, dict) else {i: None for i in lazy}
    specs = [ANY if i in rows_of else spec for i, spec in enumerate(specs)]

    def split_of(shape):
        return shape[0] if len(shape) > 2 and shape[0] in (2, 4) else 1

    buffers, sems = [], []
    for i, rows in rows_of.items():
        shape = args[i].shape if rows is None else (rows,) + args[i].shape[1:]
        buffers.append(pltpu.VMEM(shape, args[i].dtype))
        sems.append(pltpu.SemaphoreType.DMA((split_of(shape),)))
    for o in late:
        shape, dtype = outs[o]
        buffers.append(pltpu.VMEM(shape, dtype))
        sems.append(pltpu.SemaphoreType.DMA((split_of(shape),)))
    staged = len(buffers)

    def whole(*refs):
        ins, results = list(refs[:given]), list(refs[given + extra : given + extra + made])
        rest = refs[given + extra + made + len(through) :]
        held, marks, rest = rest[:staged], rest[staged : 2 * staged], rest[2 * staged :]
        coming, going, left = {}, {}, []

        def copies(source, target, mark):
            count = split_of(target.shape)
            if count == 1:
                return [pltpu.make_async_copy(source, target, mark.at[0])]
            return [
                pltpu.make_async_copy(source.at[p], target.at[p], mark.at[p]) for p in range(count)
            ]

        for (i, rows), buffer, mark in zip(rows_of.items(), held, marks):
            source = ins[i]
            if rows is not None:
                source = source.at[pl.ds(pl.multiple_of(ins[0][0] * rows, rows), rows)]
            coming[i] = copies(source, buffer, mark)
            ins[i] = buffer
        for o, buffer, mark in zip(late, held[len(rows_of) :], marks[len(rows_of) :]):
            going[o] = copies(buffer, results[o], mark)
            results[o] = buffer
        wanted = parts or {}
        for i, group in coming.items():
            for p, copy in enumerate(group):
                if p in wanted.get(i, range(len(group))):
                    copy.start()

        def arrive(i, p=0):
            coming[i][p].wait()

        def leave(o, p=0):
            going[o][p].start()
            left.append(going[o][p])

        body(types.SimpleNamespace(arrive=arrive, leave=leave), *ins, *results, *rest)
        for copy in left:
            copy.wait()

    return pl.pallas_call(
        whole,
        out_shape=[jax.ShapeDtypeStruct(shape, dtype) for shape, dtype in outs]
        + [jax.ShapeDtypeStruct(a.shape, a.dtype) for a in through],
        in_specs=list(specs) + [ANY] * extra,
        out_specs=[ANY if o in late else VMEM for o in range(made)] + [ANY] * len(through),
        scratch_shapes=buffers + sems + list(scratch),
        name=name,
        input_output_aliases={given + len(after) + n: made + n for n in range(len(through))},
        cost_estimate=pl.CostEstimate(
            flops=int(COST.get(name, 2) * 1_000_000_000), bytes_accessed=0, transcendentals=0
        ),
        compiler_params=pltpu.CompilerParams(vmem_limit_bytes=limit * MIB),
    )(*args, *after, *through)


def stack_heads(block, heads):
    lane = lax.broadcasted_iota(jnp.int32, block.shape, 1) // HEAD
    zero = jnp.zeros_like(block)
    return jnp.concatenate([jnp.where(lane == h, block, zero) for h in range(heads)], 0)


def pick_heads(stacked, heads):
    size = stacked.shape[1] // heads
    rows = [stacked[h * HEAD : (h + 1) * HEAD, h * size : (h + 1) * size] for h in range(heads)]
    return jnp.concatenate(rows, 0).T


def prepare_body(
    io, place, tokens, w_out, w_up, w_down, up_bias, b0, b1, b2, b3, b4, b5,
    high_out, low_out, own_out, half_down, rows_out, marks,
):
    rows, cols = tokens.shape[0], w_out.shape[0]
    half = half_down.shape[0]
    mine = pl.ds(pl.multiple_of((place[1] & 1) * half, half), half)
    copies = [
        pltpu.make_async_copy(source, target, marks.at[n])
        for n, (source, target) in enumerate(
            (
                (tokens.at[pl.ds(rows - MOST, MOST)], high_out),
                (tokens.at[pl.ds(0, MOST)], low_out),
                (w_out, own_out.at[pl.ds(0, cols)]),
                (w_up.at[mine], own_out.at[pl.ds(cols + 16, half)]),
                (w_down.at[mine], half_down),
            )
        )
    ]
    for copy in copies:
        copy.start()
    rest = up_bias[...].reshape(1, -1)
    pieces = []
    for _ in range(3):
        pieces.append(rest.astype(BF).astype(F32))
        rest = rest - pieces[-1]
    pieces = jnp.concatenate(pieces + [jnp.zeros((13, rest.shape[1]), F32)], 0)
    own_out[cols : cols + 16, :] = pieces.astype(BF)
    rows_out[...] = jnp.zeros_like(rows_out)
    for n, ref in enumerate((b0, b1, b2, b3, b4, b5)):
        rows_out[n : n + 1, :] = ref[...].reshape(1, -1)
    for copy in copies:
        copy.wait()


def prepare(place, tokens, w_out, w_up, w_down, up_bias, vectors):
    width = tokens.shape[1]
    half = (w_up.shape[0] // 2, width)
    return call(
        prepare_body,
        [((MOST, width), BF)] * 2
        + [((w_out.shape[0] + 16 + half[0], width), BF), (half, BF), ((8, width), F32)],
        [SMEM] + [ANY] * 4 + [VMEM] * 7,
        "prepare",
        (place, tokens, w_out, w_up, w_down, up_bias, *vectors),
        scratch=[pltpu.SemaphoreType.DMA((5,))],
    )


def project_block(block, wt, bias, target, k_out, v_out, kt_out, vt_out):
    span = pl.ds(target, block.shape[0])
    keys = nt(block, wt[1])
    k_out[span, :] = keys.astype(BF)
    kt_out[:, span] = keys.T.astype(BF)
    values = nt(block, wt[2]) + bias[1:2, :]
    v_out[span, :] = values.astype(BF)
    vt_out[:, span] = values.T.astype(BF)


def project_body(
    io, place, tokens, wt, bias, lengths, q_out, k_out, v_out, kt_out, vt_out, col_out, row_out
):
    rows = tokens.shape[0]
    ext = col_out.shape[0]
    sents = lengths.shape[1]
    step = 256

    lens = jnp.broadcast_to(lengths[...], (sents, sents))
    down = lax.broadcasted_iota(jnp.int32, (sents, sents), 0)
    across = lax.broadcasted_iota(jnp.int32, (sents, sents), 1)
    ends_col = jnp.sum(jnp.where(across <= down, lens, 0), 1, keepdims=True)
    ends_row = jnp.sum(jnp.where(down == across, ends_col, 0), 0, keepdims=True)
    first = place[1] * rows - MOST

    def sentence(at, ends, axis):
        passed = jnp.sum((ends <= at).astype(jnp.int32), axis, keepdims=True)
        return jnp.where((at < 0) | (at >= place[2]), -1, passed)

    @pl.loop(0, ext // step)
    def _(i):
        base = pl.multiple_of(i * step, step)
        at = first + base
        row_out[:, pl.ds(base, step)] = sentence(
            at + lax.broadcasted_iota(jnp.int32, (1, step), 1), ends_col, 0
        )
        col_out[pl.ds(base, step), :] = sentence(
            at + lax.broadcasted_iota(jnp.int32, (step, 1), 0), ends_row, 1
        )

    @pl.loop(0, rows // step, unroll=2)
    def _(i):
        first = pl.multiple_of(i * step, step)
        block = tokens[pl.ds(first, step), :]
        q_out[pl.ds(first, step), :] = (nt(block, wt[0]) + bias[0:1, :]).astype(BF)
        target = pl.multiple_of(first + MOST, MOST)
        project_block(block, wt, bias, target, k_out, v_out, kt_out, vt_out)


def project(place, tokens, wt, bias, lengths, after=()):
    rows, cols = tokens.shape[0], wt.shape[1]
    ext = rows + 2 * MOST
    return call(
        project_body,
        [((rows, cols), BF), ((ext, cols), BF), ((ext, cols), BF), ((cols, ext), BF), ((cols, ext), BF)]
        + [((ext, 1), jnp.int32), ((1, ext), jnp.int32)],
        [SMEM] + [VMEM] * 4,
        "project",
        (place, tokens, wt, bias, lengths),
        after,
    )


def attend_body(
    io, place, q, k_in, v_in, kt_in, vt_in, ids_col, ids_row, low, high, wt, bias,
    p_out, k_out, v_out, kt_out, m0, m1, m2, m3, vt, marks,
):
    rows, cols = q.shape
    heads = cols // HEAD
    scale = jnp.asarray(HEAD**-0.5, BF)
    per = rows // 4 // MOST
    held = (k_out, v_out, kt_out, vt)
    copies = [
        pltpu.make_async_copy(source, target, marks.at[n])
        for n, (source, target) in enumerate(zip((k_in, v_in, kt_in, vt_in), held))
    ]
    for copy in copies:
        copy.start()
    for copy in copies:
        copy.wait()
    project_block(low[...], wt, bias, 0, *held)
    project_block(high[...], wt, bias, rows + MOST, *held)
    for o in (1, 2, 3):
        io.leave(o)
    for rel, mixed_out in reversed(list(enumerate((m0, m1, m2, m3)))):

        @pl.loop(0, per, unroll=4)
        def _(i):
            b = (place[0] ^ rel) * per + i
            first = pl.multiple_of(b * MOST, MOST)
            span = pl.ds(first, 3 * MOST)
            q3 = stack_heads(q[pl.ds(first, MOST), :] * scale, heads)
            scores = nt(k_out[span, :], q3)
            mine = ids_row[:, pl.ds(pl.multiple_of(first + MOST, MOST), MOST)]
            mask = ids_col[span, :] == mine
            scores = jnp.where(jnp.concatenate([mask] * heads, 1), scores, -1e30)
            raised = jnp.exp(scores - jnp.max(scores, 0, keepdims=True))
            probs = raised * (1.0 / jnp.sum(raised, 0, keepdims=True))
            probs = probs.astype(BF)
            p_out[rel, i] = probs
            mixed = pick_heads(nn(vt[:, span], probs), heads)
            mixed_out[pl.ds(pl.multiple_of(i * MOST, MOST), MOST), :] = mixed.astype(BF)

        io.leave(0, rel)


def attend(place, q, k, v, kt, vt, ids_col, ids_row, low, high, wt, bias, after=()):
    rows, cols = q.shape
    heads = cols // HEAD
    return call(
        attend_body,
        [
            ((4, rows // 4 // MOST, 3 * MOST, heads * MOST), BF),
            (k.shape, BF),
            (v.shape, BF),
            (kt.shape, BF),
        ]
        + [((rows // 4, cols), BF)] * 4,
        [SMEM, VMEM] + [ANY] * 4 + [VMEM] * 6,
        "attend",
        (place, q, k, v, kt, vt, ids_col, ids_row, low, high, wt, bias),
        after,
        scratch=[pltpu.VMEM(vt.shape, BF), pltpu.SemaphoreType.DMA((4,))],
        late=(0, 1, 2, 3),
    )


def attend_pull(b, q, k, kt, v, p_low, grad):
    heads = q.shape[1] // HEAD
    scale = jnp.asarray(HEAD**-0.5, BF)
    first = pl.multiple_of(b * MOST, MOST)
    span = pl.ds(first, 3 * MOST)
    g_stack = stack_heads(grad, heads)
    q_stack = stack_heads(q[pl.ds(first, MOST), :] * scale, heads)
    weights = p_low.astype(F32)
    grad_probs = nt(v[span, :], g_stack)
    inner = jnp.sum(weights * grad_probs, 0, keepdims=True)
    grad_scores = (weights * (grad_probs - inner)).astype(BF)
    dq = pick_heads(nn(kt[:, span], grad_scores), heads) * (HEAD**-0.5)
    return dq, nn(grad_scores, q_stack), nn(p_low, g_stack)


def rims_body(io, place, q, k, kt, v, probs, g0, g1, g2, g3, low_out, high_out, held, grad, marks):
    quarter = g0.shape[0]
    per = quarter // MOST
    blocks = q.shape[0] // MOST
    copies = [
        pltpu.make_async_copy(probs.at[place[0] ^ far, i], held.at[n], marks.at[n])
        for n, (far, i) in enumerate(((0, 0), (3, per - 1)))
    ]
    for copy in copies:
        copy.start()
    for rel, ref in enumerate((g0, g1, g2, g3)):

        @pl.when(place[0] == rel)
        def _():
            grad[0] = ref[0:MOST, :]

        @pl.when((place[0] ^ 3) == rel)
        def _():
            grad[1] = ref[quarter - MOST :, :]

    for n, (b, out) in enumerate(((0, low_out), (blocks - 1, high_out))):
        copies[n].wait()
        _, dk, dv = attend_pull(b, q, k, kt, v, held[n], grad[n])
        here = slice(0, MOST) if n == 0 else slice(2 * MOST, 3 * MOST)
        out[0] = dk[here, :].astype(BF)
        out[1] = dv[here, :].astype(BF)


def rims(place, q, k, kt, v, probs, grads, after=()):
    cols = q.shape[1]
    return call(
        rims_body,
        [((2, MOST, cols), BF), ((2, MOST, cols), BF)],
        [SMEM] + [VMEM] * 4 + [ANY] + [VMEM] * 4,
        "rims",
        (place, q, k, kt, v, probs, *grads),
        after,
        scratch=[
            pltpu.VMEM((2,) + probs.shape[2:], BF),
            pltpu.VMEM((2, MOST, cols), BF),
            pltpu.SemaphoreType.DMA((2,)),
        ],
    )


def attend_back_body(rels, io, place, q, k, kt, v, probs, ga, gb, dq_out, dk_out, dv_out):
    quarter = ga.shape[0]
    per = quarter // MOST
    base = ((place[0] ^ rels[0]) >> 1) * (2 * per)
    dk_out[...] = jnp.zeros_like(dk_out)
    dv_out[...] = jnp.zeros_like(dv_out)
    for n, (rel, ref) in enumerate(zip(rels, (ga, gb))):
        io.arrive(5, rel)

        @pl.loop(0, per, unroll=4)
        def _(i):
            b = (place[0] ^ rel) * per + i
            rows = pl.ds(pl.multiple_of(i * MOST, MOST), MOST)
            dq, dk, dv = attend_pull(b, q, k, kt, v, probs[rel, i], ref[rows, :])
            dq_out[n, rows, :] = dq.astype(BF)
            span = pl.ds(pl.multiple_of((b - base) * MOST, MOST), 3 * MOST)
            dk_out[span, :] += dk
            dv_out[span, :] += dv


def attend_back(rels, place, q, k, kt, v, probs, grads, after=(), through=()):
    rows, cols = q.shape
    half = rows // 2 + 2 * MOST
    return call(
        functools.partial(attend_back_body, rels),
        [((2, rows // 4, cols), BF), ((half, cols), F32), ((half, cols), F32)],
        [SMEM] + [VMEM] * 7,
        "attend_back",
        (place, q, k, kt, v, probs, *grads),
        after,
        through,
        lazy=(5,),
        parts={5: rels},
    )


def input_back_body(
    io, place, dqa, dqb, dka, dkb, dva, dvb, from_low, from_high, wt, kv, keep_out, send_out, sums
):
    rows = kv.shape[1]
    quarter, half = rows // 4, rows // 2
    sums[...] = jnp.zeros_like(sums)
    for side, refs in enumerate(((dka, dva), (dkb, dvb))):
        here = pl.ds(pl.multiple_of(((place[0] >> 1) ^ side) * half, half), half + 2 * MOST)
        for j, ref in enumerate(refs):
            sums[j, here, :] += ref[...]
    for j in range(2):
        sums[j, MOST : 2 * MOST, :] += from_low[j].astype(F32)
        sums[j, rows : rows + MOST, :] += from_high[j].astype(F32)
        kv[j] = sums[j, MOST : rows + MOST, :].astype(BF)
    dq = [dqa.at[0], dqa.at[1], dqb.at[0], dqb.at[1]]
    for rel in (1, 3, 0, 2):
        here = pl.ds(pl.multiple_of((place[0] ^ rel) * quarter, quarter), quarter)
        part = nn(dq[rel][...], wt[0]) + nn(kv[0, here, :], wt[1]) + nn(kv[1, here, :], wt[2])
        out = send_out if rel % 2 else keep_out
        out[rel // 2] = part.astype(out.dtype)


def input_back(place, firsts, seconds, from_low, from_high, wt, rows, after=(), through=()):
    cols, width = wt.shape[1], wt.shape[2]
    pairs = [a for pair in zip(firsts, seconds) for a in pair]
    return call(
        input_back_body,
        [
            ((2, rows, cols), BF),
            ((2, rows // 4, width), F32),
            ((2, rows // 4, width), BF),
        ],
        [SMEM] + [VMEM] * 9,
        "input_back",
        (place, *pairs, from_low, from_high, wt),
        after,
        through,
        scratch=[pltpu.VMEM((2, rows + 2 * MOST, cols), F32)],
    )


def qkv_grads_body(io, place, tokens, dqa, dqb, kv, dwt):
    rows = tokens.shape[0]
    cols = kv.shape[2]
    quarter = rows // 4
    total = 0
    for rel, d in enumerate((dqa.at[0], dqa.at[1], dqb.at[0], dqb.at[1])):
        here = pl.ds(pl.multiple_of((place[0] ^ rel) * quarter, quarter), quarter)
        total = total + tn(d[...], tokens[here, :])
    dwt[0:cols, :] = total
    dwt[cols : 2 * cols, :] = tn(kv[0], tokens[...])
    dwt[2 * cols : 3 * cols, :] = tn(kv[1], tokens[...])
    dwt[3 * cols :, :] = jnp.zeros_like(dwt[3 * cols :, :])
    sums = [col_sum(d[n].astype(F32)) for d in (dqa, dqb) for n in range(2)]
    dwt[3 * cols : 3 * cols + 1, 0:cols] = sum(sums)
    dwt[3 * cols + 1 : 3 * cols + 2, 0:cols] = col_sum(kv[1].astype(F32))


def qkv_grads(place, tokens, dqa, dqb, kv, after=(), through=()):
    cols, width = kv.shape[2], tokens.shape[1]
    return call(
        qkv_grads_body,
        [((3 * cols + PAD, width), F32)],
        [SMEM] + [VMEM] * 4,
        "qkv_grads",
        (place, tokens, dqa, dqb, kv),
        after,
        through,
    )


def gelu_parts(pre):
    size = jnp.abs(pre) * (0.5**0.5)
    bell = jnp.exp(-size * size)
    t = 1.0 / (1.0 + 0.3275911 * size)
    poly = 1.061405429
    for c in (-1.453152027, 1.421413741, -0.284496736, 0.254829592):
        poly = poly * t + c
    tail = 0.5 * poly * t * bell
    cdf = jnp.where(pre >= 0, 1.0 - tail, tail)
    return pre * cdf, cdf + pre * bell * 0.3989422804014327


def norm_stats(resid):
    centred = resid - jnp.mean(resid, -1, keepdims=True)
    inv = lax.rsqrt(jnp.mean(centred * centred, -1, keepdims=True) + EPS)
    return centred * inv, inv


def norm_pull(grad, normed, inv, gain):
    scaled = grad * gain
    return inv * (
        scaled
        - jnp.mean(scaled, -1, keepdims=True)
        - normed * jnp.mean(scaled * normed, -1, keepdims=True)
    )


def col_sum(values):
    return jnp.sum(values, 0, keepdims=True)


STEP = 256
PAD = 64
OUT_BIAS, GAIN1, SHIFT1, DOWN_BIAS, GAIN2, SHIFT2 = range(6)


def forward_body(
    io, place, tokens, m0, m1, m2, m3, o0, o1, o2, o3, u0, u1, u2, u3, rows_in,
    normed_out, inv_out, low_out, act_out, slope_out,
):
    cols = m0.shape[1]
    attn = rows_in[OUT_BIAS : OUT_BIAS + 1, :]
    for rel, (m, o) in enumerate(((m0, o0), (m1, o1), (m2, o2), (m3, o3))):
        io.arrive(2 + rel)
        io.arrive(6 + rel)
        attn = attn + nn(m[...], o[0:cols, :])
    io.arrive(1)
    normed, inv = norm_stats(tokens[...].astype(F32) + attn)
    normed_out[...] = normed
    inv_out[...] = inv
    low_out[...] = (normed * rows_in[GAIN1 : GAIN1 + 1, :] + rows_in[SHIFT1 : SHIFT1 + 1, :]).astype(BF)
    io.leave(0)
    io.leave(2)
    for rel, (u, o) in enumerate(((u0, o0), (u1, o1), (u2, o2), (u3, o3))):
        io.arrive(10 + rel)

        @pl.loop(0, u.shape[1] // STEP, unroll=3)
        def _(j):
            here = pl.ds(pl.multiple_of(j * STEP, STEP), STEP)
            bias = col_sum(o[cols : cols + 16, here].astype(F32))
            act, slope = gelu_parts(nn(low_out[...], u[:, here]) + bias)
            act_out[rel, :, here] = act.astype(BF)
            slope_out[rel, :, here] = slope.astype(BF)

        io.leave(3, rel)
        io.leave(4, rel)


def forward(place, tokens, mixed, outs, ups, rows_in, after=()):
    rows, width = tokens.shape[0] // 4, tokens.shape[1]
    hidden = ups[0].shape[1]
    return call(
        forward_body,
        [
            ((rows, width), F32),
            ((rows, 1), F32),
            ((rows, width), BF),
            ((4, rows, hidden), BF),
            ((4, rows, hidden), BF),
        ],
        [SMEM] + [VMEM] * 14,
        "forward",
        (place, tokens, *mixed, *outs, *ups, rows_in),
        after,
        lazy={1: rows, **{i: None for i in range(2, 14)}},
        late=(0, 2, 3, 4),
    )


def middle_body(
    io, place, normed1, act, w0, w1, w2, w3, cot, rows_in,
    result_out, res2_out, low_out, keep_out, send_out, sums_out,
):
    down = rows_in[DOWN_BIAS : DOWN_BIAS + 1, :]
    for rel, w in enumerate((w0, w1, w2, w3)):
        io.arrive(2, rel)
        io.arrive(3 + rel)
        down = down + nn(act[rel], w[...])
    io.arrive(1)
    first = normed1[...] * rows_in[GAIN1 : GAIN1 + 1, :] + rows_in[SHIFT1 : SHIFT1 + 1, :]
    gain2 = rows_in[GAIN2 : GAIN2 + 1, :]
    normed, inv = norm_stats(first + down)
    result_out[...] = (normed * gain2 + rows_in[SHIFT2 : SHIFT2 + 1, :]).astype(BF)
    io.leave(0)
    io.arrive(7)
    grad = cot[...].astype(F32)
    res2 = norm_pull(grad, normed, inv, gain2)
    res2_out[...] = res2
    io.leave(1)
    low = res2.astype(BF)
    low_out[...] = low
    io.leave(2)
    sums_out[0:1, :] = col_sum(grad * normed)
    sums_out[1:2, :] = col_sum(grad)
    sums_out[2:3, :] = col_sum(low.astype(F32))
    for rel in (1, 3, 0, 2):
        out, o = (send_out, 4) if rel % 2 else (keep_out, 3)
        out[rel // 2] = tn(act[rel], low_out[...]).astype(BF)
        io.leave(o, rel // 2)


def middle(place, normed1, act, downs, cot, rows_in, after=()):
    rows, width = normed1.shape
    hidden = act.shape[2]
    return call(
        middle_body,
        [
            ((rows, width), BF),
            ((rows, width), F32),
            ((rows, width), BF),
            ((2, hidden, width), BF),
            ((2, hidden, width), BF),
            ((3, width), F32),
        ],
        [SMEM] + [VMEM] * 8,
        "middle",
        (place, normed1, act, *downs, cot, rows_in),
        after,
        lazy={2: None, 3: None, 4: None, 5: None, 6: None, 1: None, 7: rows},
        late=(0, 1, 2, 3, 4),
    )


def backward_body(
    io, low2, res2, normed1, inv1, slope, w0, w1, w2, w3, u0, u1, u2, u3, o0, o1, o2, o3, rows_in,
    gup_out, res1_out, low_out, gm0, gm1, gm2, gm3, sums_out, ups_out, total,
):
    cols = gm0.shape[1]
    for rel, (w, u) in enumerate(((w0, u0), (w1, u1), (w2, u2), (w3, u3))):

        @pl.loop(0, u.shape[1] // STEP, unroll=3)
        def _(j):
            here = pl.ds(pl.multiple_of(j * STEP, STEP), STEP)
            grad_act = nt(low2[...], w[here, :])
            low = (grad_act * slope[rel, :, here].astype(F32)).astype(BF)
            gup_out[rel, :, here] = low
            ups_out[rel : rel + 1, here] = col_sum(low.astype(F32))
        total[...] = (res2 if rel == 0 else total)[...] + nt(gup_out[rel], u[...])
    grad = total[...]
    res1 = norm_pull(grad, normed1[...], inv1[...], rows_in[GAIN1 : GAIN1 + 1, :])
    res1_out[...] = res1
    low = res1.astype(BF)
    low_out[...] = low
    sums_out[0:1, :] = col_sum(grad * normed1[...])
    sums_out[1:2, :] = col_sum(grad)
    sums_out[2:3, :] = col_sum(low.astype(F32))
    for rel, (gm_out, o) in enumerate(zip((gm0, gm1, gm2, gm3), (o0, o1, o2, o3))):
        gm_out[...] = nt(low, o[0:cols, :]).astype(BF)


def backward(low2, res2, normed1, inv1, slope, downs, ups, outs, rows_in, cols, after=()):
    rows, width = low2.shape
    hidden = slope.shape[2]
    return call(
        backward_body,
        [
            ((4, rows, hidden), BF),
            ((rows, width), F32),
            ((rows, width), BF),
        ]
        + [((rows, cols), BF)] * 4
        + [
            ((3, width), F32),
            ((4, hidden), F32),
        ],
        [VMEM] * 18,
        "backward",
        (low2, res2, normed1, inv1, slope, *downs, *ups, *outs, rows_in),
        after,
        scratch=[pltpu.VMEM((rows, width), F32)],
    )


def up_grads_body(io, low1, gup, keep_out, send_out):
    for rel in (1, 3, 0, 2):
        out = send_out if rel % 2 else keep_out
        out[rel // 2] = tn(low1[:, 0 : out.shape[1]], gup[rel]).astype(BF)


def up_grads(low1, gup, first, after=()):
    return call(
        up_grads_body,
        [((2, first, gup.shape[2]), BF)] * 2,
        [VMEM] * 2,
        "up_grads",
        (low1, gup),
        after,
    )


def out_grads_body(io, low1, gup, grad_low, m0, m1, m2, m3, sums1, sums2, ups, keep_out, send_out):
    width, cols = low1.shape[1], m0.shape[1]
    left = keep_out.shape[1] - cols - PAD
    mixed = (m0, m1, m2, m3)
    for rel in (1, 3, 0, 2):
        out = send_out if rel % 2 else keep_out
        out[rel // 2, 0:left, :] = tn(low1[:, width - left :], gup[rel]).astype(BF)
        out[rel // 2, left : left + cols, :] = tn(mixed[rel][...], grad_low[...]).astype(BF)
        rows = jnp.concatenate([sums2[...], sums1[...], ups[rel : rel + 1, :]], 0)
        rows = jnp.concatenate([rows, jnp.zeros((PAD - rows.shape[0], width), F32)], 0)
        out[rel // 2, left + cols :, :] = rows.astype(BF)


def out_grads(low1, gup, grad_low, mixed, sums1, sums2, ups, left, after=()):
    hidden = gup.shape[2]
    cols = mixed[0].shape[1]
    return call(
        out_grads_body,
        [((2, left + cols + PAD, hidden), BF)] * 2,
        [VMEM] * 10,
        "out_grads",
        (low1, gup, grad_low, *mixed, sums1, sums2, ups),
        after,
    )


def place_rows_body(io, place, p0, p1, p2, p3, out):
    quarter = p0.shape[0]
    for rel, p in enumerate((p0, p1, p2, p3)):
        here = pl.ds(pl.multiple_of((place[0] ^ rel) * quarter, quarter), quarter)
        out[here, :] = p[...].astype(out.dtype)


def place_rows(place, parts, dtype, after=()):
    quarter, width = parts[0].shape
    return call(
        place_rows_body,
        [((4 * quarter, width), dtype)],
        [SMEM] + [VMEM] * 4,
        "place_rows",
        (place, *parts),
        after,
    )[0]


def swap(value, axis, bits):
    count = lax.axis_size(axis)
    return lax.ppermute(value, axis, [(i, i ^ bits) for i in range(count)])


def gather_rel(own):
    far = swap(own, "tp", 2)
    return (own, swap(own, "tp", 1), far, swap(far, "tp", 1))


def core_sum(keep, got):
    two = keep.astype(F32) + got.astype(F32)
    return two[0].astype(BF), two[1].astype(BF)


def total(keep, got):
    return keep.astype(F32) + got.astype(F32)


def divide(part, level):
    return divide_sum((part,), level)


def divide_sum(parts, level):
    half = parts[0].shape[0] // 2
    first = ((lax.axis_index("seq") >> level) & 1) * half
    send = sum(lax.dynamic_slice_in_dim(p, half - first, half, 0).astype(F32) for p in parts)
    keep = sum(lax.dynamic_slice_in_dim(p, first, half, 0).astype(F32) for p in parts)
    return send.astype(BF), keep


def join(part, other, level):
    upper = ((lax.axis_index("seq") >> level) & 1) != 0
    return jnp.where(
        upper, jnp.concatenate([other, part], 0), jnp.concatenate([part, other], 0)
    )


class Line:
    def __init__(self, first):
        self.last = first

    def take(self, *arrays):
        *arrays, _ = lax.optimization_barrier((*arrays, self.last))
        return arrays if len(arrays) > 1 else arrays[0]

    def put(self, *arrays):
        self.last = arrays[0]
        return arrays if len(arrays) > 1 else arrays[0]


class SeqSum:
    def __init__(self, line, bits):
        self.line, self.bits = line, bits

    def first(self, own, far=None):
        parts = [self.line.take(own)] if far is None else self.line.take(own, far)
        send, self.keep = self.line.put(*divide_sum(parts, self.bits[0]))
        self.got = swap(send, "seq", 1 << self.bits[0])

    def second(self):
        parts = self.line.take(self.keep, self.got)
        send, self.keep = self.line.put(*divide_sum(parts, self.bits[1]))
        self.got = swap(send, "seq", 1 << self.bits[1])

    def third(self):
        part = self.line.put(total(*self.line.take(self.keep, self.got)).astype(BF))
        levels = lax.axis_size("seq").bit_length() - 1
        for k in range(2, levels - 1):
            part = total(part, swap(part, "seq", 1 << k)).astype(BF)
        self.keep, self.got = part, swap(part, "seq", 1 << (levels - 1))

    def fourth(self):
        self.keep = self.line.put(total(*self.line.take(self.keep, self.got)).astype(BF))
        self.got = swap(self.keep, "seq", 1 << self.bits[1])

    def fifth(self):
        self.keep = self.line.put(join(*self.line.take(self.keep, self.got), self.bits[1]))
        self.got = swap(self.keep, "seq", 1 << self.bits[0])

    def sixth(self):
        return self.line.put(join(*self.line.take(self.keep, self.got), self.bits[0]).astype(F32))


def on_device(
    tokens, cotangent, lengths, w_qkv, qv_bias, w_out, out_bias, gain_first, shift_first,
    w_up, up_bias, w_down, down_bias, gain_second, shift_second,
):
    rows, width = tokens.shape
    quarter = rows // 4
    cols = w_qkv.shape[2]
    hidden = w_up.shape[1]
    seq_count = lax.axis_size("seq")
    tp_place = lax.axis_index("tp")
    seq_place = lax.axis_index("seq")
    place = jnp.stack([tp_place, seq_place, rows * seq_count]).astype(jnp.int32)
    forwards = [(i, i + 1) for i in range(seq_count - 1)]
    backwards = [(b, a) for a, b in forwards]

    vectors = [out_bias, gain_first, shift_first, down_bias, gain_second, shift_second]
    high, low, bundle, half_d, rows_in = prepare(
        place, tokens, w_out, w_up, w_down, up_bias, vectors
    )
    low, high = lax.ppermute(high, "seq", forwards), lax.ppermute(low, "seq", backwards)
    own_o = bundle[: cols + 16]
    bundle, half_d = swap(bundle, "tp", 2), swap(half_d, "tp", 2)
    wt = jnp.transpose(w_qkv, (0, 2, 1))
    q, k, v, kt, vt, ids_col, ids_row = project(
        place, tokens, wt, qv_bias, lengths.reshape(1, -1), (rows_in,)
    )
    own_o, own_u, own_d, _ = lax.optimization_barrier((own_o, w_up, w_down, q))
    near_o, near_u, near_d = [swap(a, "tp", 1) for a in (own_o, own_u, own_d)]
    probs, k, v, kt, *mixed = attend(
        place, q, k, v, kt, vt, ids_col, ids_row, low, high, wt, qv_bias
    )
    mixed = [mixed[0]] + [swap(mixed[r], "tp", r) for r in (1, 2, 3)]
    line = Line(probs)
    bundle = line.take(bundle)
    far_o, half_u = line.put(bundle[: cols + 16], bundle[cols + 16 :])
    other_u = swap(half_u, "seq", 1)
    half_d = line.put(line.take(half_d))
    other_d = swap(half_d, "seq", 1)
    last_o = swap(far_o, "tp", 1)
    mixed = line.put(*line.take(*mixed))
    far_u = line.put(join(*line.take(half_u, other_u), 0))
    last_u = swap(far_u, "tp", 1)
    outs, ups = (own_o, near_o, far_o, last_o), (own_u, near_u, far_u, last_u)
    normed1, inv1, low1, act, slope = forward(place, tokens, mixed, outs, ups, rows_in)
    far_d = join(half_d, other_d, 0)
    downs = (own_d, near_d, far_d, swap(far_d, "tp", 1))
    result, res2, low2, keep_d, send_d, sums2 = middle(
        place, normed1, act, downs, cotangent, rows_in
    )
    act_far, act_near = swap(result, "tp", 2), swap(result, "tp", 1)
    got_d = swap(send_d, "tp", 1)
    gup, res1, grad_low, g0, g1, g2, g3, sums1, up_sums = backward(
        low2, res2, normed1, inv1, slope, downs, ups, outs, rows_in, cols
    )
    g1, g2, g3 = swap(g1, "tp", 1), swap(g2, "tp", 2), swap(g3, "tp", 3)
    own_d, far_d = core_sum(keep_d, got_d)
    left = width - 512
    keep_u, send_u = up_grads(low1, gup, width - left, (own_d, far_d, act_far, act_near, g1))
    keep_v, send_v = out_grads(low1, gup, grad_low, mixed, sums1, sums2, up_sums, left, (keep_u,))
    line = Line(keep_v)
    sum_d, sum_q, sum_u, sum_v = [
        SeqSum(line, bits) for bits in ((0, 1), (1, 0), (1, 0), (0, 1))
    ]
    firsts = attend_back((0, 1), place, q, k, kt, v, probs, (g0, g1), (keep_v,))
    line.put(firsts[0])
    sum_d.first(own_d, swap(far_d, "tp", 2))
    low_rim, high_rim = rims(
        place, q, k, kt, v, probs, (g0, g1, g2, g3), (line.last,)
    )
    line.put(low_rim)
    from_high = lax.ppermute(low_rim, "seq", backwards)
    from_low = lax.ppermute(high_rim, "seq", forwards)
    own_u, far_u = line.put(*core_sum(*line.take(keep_u, swap(send_u, "tp", 1))))
    *seconds, sum_d.keep = attend_back(
        (2, 3), place, q, k, kt, v, probs, (g2, g3), (from_low, from_high, line.last),
        (sum_d.keep,),
    )
    line.put(seconds[0])
    own_v, far_v = line.put(*core_sum(*line.take(keep_v, swap(send_v, "tp", 1))))
    sum_d.second()
    kv, keep_i, send_i, own_u = input_back(
        place, firsts, seconds, from_low, from_high, wt, rows, (line.last,), (own_u,)
    )
    line.put(kv)
    sum_u.first(own_u, swap(far_u, "tp", 2))
    dwt, sum_d.keep, sum_u.keep, own_v, keep_i = qkv_grads(
        place, tokens, firsts[0], seconds[0], kv, (line.last,), (sum_d.keep, sum_u.keep, own_v, keep_i)
    )
    line.put(dwt)
    keep_i, got_i = line.take(keep_i, swap(send_i, "tp", 1))
    two = line.put(keep_i + got_i.astype(F32))
    far_i = swap(two[1].astype(BF), "tp", 2)
    sum_q.first(dwt)
    sum_d.third()
    sum_v.first(own_v, swap(far_v, "tp", 2))
    sum_u.second()
    sum_q.second()
    sum_d.fourth()
    sum_v.second()
    sum_u.third()
    far_i = line.take(far_i)
    part = line.put((two[0] + far_i.astype(F32) + res1).astype(BF))
    part_far, part_near = swap(part, "tp", 2), swap(part, "tp", 1)
    sum_q.third()
    sum_d.fifth()
    sum_u.fourth()
    sum_v.third()
    sum_q.fourth()
    sum_u.fifth()
    grad_down = sum_d.sixth()
    part_far = line.put(line.take(part_far))
    part_last = swap(part_far, "tp", 1)
    sum_v.fourth()
    sum_q.fifth()
    grad_up = sum_u.sixth()
    act_last = swap(line.take(act_far), "tp", 1)
    sum_v.fifth()
    input_grad = place_rows(place, line.take(part, part_near, part_far, part_last), F32)
    line.put(input_grad)
    result = place_rows(place, line.take(result, act_near, act_far, act_last), BF)
    line.put(result)
    grad_qkv = sum_q.sixth()
    grad_rest = sum_v.sixth()
    qv_sums = grad_qkv[3 * cols : 3 * cols + 2, :cols]
    grad_qkv = jnp.transpose(grad_qkv[: 3 * cols].reshape(3, cols, width), (0, 2, 1))
    grad_up = jnp.concatenate([grad_up, grad_rest[:left]], 0)
    grad_out = grad_rest[left : left + cols]
    sums = grad_rest[left + cols :]
    return (
        result, input_grad, grad_qkv, qv_sums, grad_out, sums[5], sums[3], sums[4],
        grad_up, sums[6], grad_down, sums[2], sums[0], sums[1],
    )


def solution(mesh):
    rep, rows = P(), P("seq", None)
    return jax.shard_map(
        on_device,
        mesh=mesh,
        in_specs=(
            rows, rows, rep, P(None, None, "tp"), P(None, "tp"), P("tp", None), rep, rep, rep,
            P(None, "tp"), P("tp"), P("tp", None), rep, rep, rep,
        ),
        out_specs=(
            rows, rows, P(None, None, "tp"), P(None, "tp"), P("tp", None), rep, rep, rep,
            P(None, "tp"), P("tp"), P("tp", None), rep, rep, rep,
        ),
        check_vma=False,
    )
```

```python
import functools
import types

import jax
import jax.numpy as jnp
from jax import lax
from jax.experimental import pallas as pl
from jax.experimental.pallas import tpu as pltpu
from jax.sharding import PartitionSpec as P

HEAD = 64
MOST = 128
EPS = 1e-12
BF = jnp.bfloat16
F32 = jnp.float32
MIB = 1024 * 1024


def nn(left, right):
    return lax.dot_general(left, right, (((1,), (0,)), ((), ())), preferred_element_type=F32)


def nt(left, right):
    return lax.dot_general(left, right, (((1,), (1,)), ((), ())), preferred_element_type=F32)


def tn(left, right):
    return lax.dot_general(left, right, (((0,), (0,)), ((), ())), preferred_element_type=F32)


VMEM = pl.BlockSpec(memory_space=pltpu.VMEM)
SMEM = pl.BlockSpec(memory_space=pltpu.SMEM)


COST = {
    "prepare": 2, "project": 3, "attend_far": 3, "attend_near": 3, "forward": 6, "middle": 5, "backward": 6, "place_rows": 2, "up_grads": 0.5, "out_grads": 0.5, "attend_back": 1, "qkv_grads": 1, "input_back": 3, "place_low": 4,
}
ANY = pl.BlockSpec(memory_space=pl.ANY)


def call(
    body, outs, specs, name, args, after=(), through=(), scratch=(), limit=56, lazy=(), late=()
):
    given, extra, made = len(args), len(after) + len(through), len(outs)
    rows_of = dict(lazy) if isinstance(lazy, dict) else {i: None for i in lazy}
    specs = [ANY if i in rows_of else spec for i, spec in enumerate(specs)]

    def split_of(shape):
        return shape[0] if len(shape) > 2 and shape[0] in (2, 4) else 1

    buffers, sems = [], []
    for i, rows in rows_of.items():
        shape = args[i].shape if rows is None else (rows,) + args[i].shape[1:]
        buffers.append(pltpu.VMEM(shape, args[i].dtype))
        sems.append(pltpu.SemaphoreType.DMA((split_of(shape),)))
    for o in late:
        shape, dtype = outs[o]
        buffers.append(pltpu.VMEM(shape, dtype))
        sems.append(pltpu.SemaphoreType.DMA((split_of(shape),)))
    staged = len(buffers)

    def whole(*refs):
        ins, results = list(refs[:given]), list(refs[given + extra : given + extra + made])
        rest = refs[given + extra + made + len(through) :]
        held, marks, rest = rest[:staged], rest[staged : 2 * staged], rest[2 * staged :]
        coming, going, left = {}, {}, []

        def copies(source, target, mark):
            count = split_of(target.shape)
            if count == 1:
                return [pltpu.make_async_copy(source, target, mark.at[0])]
            return [
                pltpu.make_async_copy(source.at[p], target.at[p], mark.at[p]) for p in range(count)
            ]

        for (i, rows), buffer, mark in zip(rows_of.items(), held, marks):
            source = ins[i]
            if rows is not None:
                source = source.at[pl.ds(pl.multiple_of(ins[0][0] * rows, rows), rows)]
            coming[i] = copies(source, buffer, mark)
            ins[i] = buffer
        for o, buffer, mark in zip(late, held[len(rows_of) :], marks[len(rows_of) :]):
            going[o] = copies(buffer, results[o], mark)
            results[o] = buffer
        for group in coming.values():
            for copy in group:
                copy.start()

        def arrive(i, p=0):
            coming[i][p].wait()

        def leave(o, p=0):
            going[o][p].start()
            left.append(going[o][p])

        body(types.SimpleNamespace(arrive=arrive, leave=leave), *ins, *results, *rest)
        for copy in left:
            copy.wait()

    return pl.pallas_call(
        whole,
        out_shape=[jax.ShapeDtypeStruct(shape, dtype) for shape, dtype in outs]
        + [jax.ShapeDtypeStruct(a.shape, a.dtype) for a in through],
        in_specs=list(specs) + [ANY] * extra,
        out_specs=[ANY if o in late else VMEM for o in range(made)] + [ANY] * len(through),
        scratch_shapes=buffers + sems + list(scratch),
        name=name,
        input_output_aliases={given + len(after) + n: made + n for n in range(len(through))},
        cost_estimate=pl.CostEstimate(
            flops=int(COST.get(name, 2) * 1_000_000_000), bytes_accessed=0, transcendentals=0
        ),
        compiler_params=pltpu.CompilerParams(vmem_limit_bytes=limit * MIB),
    )(*args, *after, *through)


def stack_heads(block, heads):
    lane = lax.broadcasted_iota(jnp.int32, block.shape, 1) // HEAD
    zero = jnp.zeros_like(block)
    return jnp.concatenate([jnp.where(lane == h, block, zero) for h in range(heads)], 0)


def pick_heads(stacked, heads):
    size = stacked.shape[1] // heads
    rows = [stacked[h * HEAD : (h + 1) * HEAD, h * size : (h + 1) * size] for h in range(heads)]
    return jnp.concatenate(rows, 0).T


def prepare_body(
    io, place, tokens, w_out, w_up, w_down, up_bias, b0, b1, b2, b3, b4, b5,
    high_out, low_out, own_out, half_down, rows_out, marks,
):
    rows, cols = tokens.shape[0], w_out.shape[0]
    half = half_down.shape[0]
    mine = pl.ds(pl.multiple_of((place[1] & 1) * half, half), half)
    copies = [
        pltpu.make_async_copy(source, target, marks.at[n])
        for n, (source, target) in enumerate(
            (
                (tokens.at[pl.ds(rows - MOST, MOST)], high_out),
                (tokens.at[pl.ds(0, MOST)], low_out),
                (w_out, own_out.at[pl.ds(0, cols)]),
                (w_up.at[mine], own_out.at[pl.ds(cols + 16, half)]),
                (w_down.at[mine], half_down),
            )
        )
    ]
    for copy in copies:
        copy.start()
    rest = up_bias[...].reshape(1, -1)
    pieces = []
    for _ in range(3):
        pieces.append(rest.astype(BF).astype(F32))
        rest = rest - pieces[-1]
    pieces = jnp.concatenate(pieces + [jnp.zeros((13, rest.shape[1]), F32)], 0)
    own_out[cols : cols + 16, :] = pieces.astype(BF)
    rows_out[...] = jnp.zeros_like(rows_out)
    for n, ref in enumerate((b0, b1, b2, b3, b4, b5)):
        rows_out[n : n + 1, :] = ref[...].reshape(1, -1)
    for copy in copies:
        copy.wait()


def prepare(place, tokens, w_out, w_up, w_down, up_bias, vectors):
    width = tokens.shape[1]
    half = (w_up.shape[0] // 2, width)
    return call(
        prepare_body,
        [((MOST, width), BF)] * 2
        + [((w_out.shape[0] + 16 + half[0], width), BF), (half, BF), ((8, width), F32)],
        [SMEM] + [ANY] * 4 + [VMEM] * 7,
        "prepare",
        (place, tokens, w_out, w_up, w_down, up_bias, *vectors),
        scratch=[pltpu.SemaphoreType.DMA((5,))],
    )


def project_block(block, wt, bias, target, k_out, v_out, kt_out, vt_out):
    span = pl.ds(target, block.shape[0])
    keys = nt(block, wt[1])
    k_out[span, :] = keys.astype(BF)
    kt_out[:, span] = keys.T.astype(BF)
    values = nt(block, wt[2]) + bias[1:2, :]
    v_out[span, :] = values.astype(BF)
    vt_out[:, span] = values.T.astype(BF)


def project_body(
    io, place, tokens, wt, bias, lengths, q_out, k_out, v_out, kt_out, vt_out, col_out, row_out
):
    rows = tokens.shape[0]
    ext = col_out.shape[0]
    sents = lengths.shape[1]
    step = 256

    lens = jnp.broadcast_to(lengths[...], (sents, sents))
    down = lax.broadcasted_iota(jnp.int32, (sents, sents), 0)
    across = lax.broadcasted_iota(jnp.int32, (sents, sents), 1)
    ends_col = jnp.sum(jnp.where(across <= down, lens, 0), 1, keepdims=True)
    ends_row = jnp.sum(jnp.where(down == across, ends_col, 0), 0, keepdims=True)
    first = place[1] * rows - MOST

    def sentence(at, ends, axis):
        passed = jnp.sum((ends <= at).astype(jnp.int32), axis, keepdims=True)
        return jnp.where((at < 0) | (at >= place[2]), -1, passed)

    @pl.loop(0, ext // step)
    def _(i):
        base = pl.multiple_of(i * step, step)
        at = first + base
        row_out[:, pl.ds(base, step)] = sentence(
            at + lax.broadcasted_iota(jnp.int32, (1, step), 1), ends_col, 0
        )
        col_out[pl.ds(base, step), :] = sentence(
            at + lax.broadcasted_iota(jnp.int32, (step, 1), 0), ends_row, 1
        )

    @pl.loop(0, rows // step, unroll=2)
    def _(i):
        first = pl.multiple_of(i * step, step)
        block = tokens[pl.ds(first, step), :]
        q_out[pl.ds(first, step), :] = (nt(block, wt[0]) + bias[0:1, :]).astype(BF)
        target = pl.multiple_of(first + MOST, MOST)
        project_block(block, wt, bias, target, k_out, v_out, kt_out, vt_out)


def project(place, tokens, wt, bias, lengths, after=()):
    rows, cols = tokens.shape[0], wt.shape[1]
    ext = rows + 2 * MOST
    return call(
        project_body,
        [((rows, cols), BF), ((ext, cols), BF), ((ext, cols), BF), ((cols, ext), BF), ((cols, ext), BF)]
        + [((ext, 1), jnp.int32), ((1, ext), jnp.int32)],
        [SMEM] + [VMEM] * 4,
        "project",
        (place, tokens, wt, bias, lengths),
        after,
    )


def attend_quarters(io, rels, place, q, k, vt, ids_col, ids_row, p_out, mixed_outs):
    rows, cols = q.shape
    heads = cols // HEAD
    scale = jnp.asarray(HEAD**-0.5, BF)
    per = rows // 4 // MOST
    for n, (rel, mixed_out) in enumerate(zip(rels, mixed_outs)):

        @pl.loop(0, per, unroll=4)
        def _(i):
            b = (place[0] ^ rel) * per + i
            first = pl.multiple_of(b * MOST, MOST)
            span = pl.ds(first, 3 * MOST)
            q3 = stack_heads(q[pl.ds(first, MOST), :] * scale, heads)
            scores = nt(k[span, :], q3)
            mine = ids_row[:, pl.ds(pl.multiple_of(first + MOST, MOST), MOST)]
            mask = ids_col[span, :] == mine
            scores = jnp.where(jnp.concatenate([mask] * heads, 1), scores, -1e30)
            raised = jnp.exp(scores - jnp.max(scores, 0, keepdims=True))
            probs = raised * (1.0 / jnp.sum(raised, 0, keepdims=True))
            probs = probs.astype(BF)
            p_out[n, i] = probs
            mixed = pick_heads(nn(vt[:, span], probs), heads)
            mixed_out[pl.ds(pl.multiple_of(i * MOST, MOST), MOST), :] = mixed.astype(BF)

        io.leave(0, n)


def attend_far_body(
    io, place, q, k_in, v_in, kt_in, vt_in, ids_col, ids_row, low, high, wt, bias,
    p_out, k_out, v_out, kt_out, vt_out, m0, m1, marks,
):
    rows = q.shape[0]
    held = (k_out, v_out, kt_out, vt_out)
    copies = [
        pltpu.make_async_copy(source, target, marks.at[n])
        for n, (source, target) in enumerate(zip((k_in, v_in, kt_in, vt_in), held))
    ]
    for copy in copies:
        copy.start()
    for copy in copies:
        copy.wait()
    project_block(low[...], wt, bias, 0, *held)
    project_block(high[...], wt, bias, rows + MOST, *held)
    for o in (1, 2, 3, 4):
        io.leave(o)
    attend_quarters(io, (2, 3), place, q, k_out, vt_out, ids_col, ids_row, p_out, (m0, m1))


def attend_far(place, q, k, v, kt, vt, ids_col, ids_row, low, high, wt, bias, after=()):
    rows, cols = q.shape
    heads = cols // HEAD
    return call(
        attend_far_body,
        [((2, rows // 4 // MOST, 3 * MOST, heads * MOST), BF)]
        + [(a.shape, BF) for a in (k, v, kt, vt)]
        + [((rows // 4, cols), BF)] * 2,
        [SMEM, VMEM] + [ANY] * 4 + [VMEM] * 6,
        "attend_far",
        (place, q, k, v, kt, vt, ids_col, ids_row, low, high, wt, bias),
        after,
        scratch=[pltpu.SemaphoreType.DMA((4,))],
        late=(0, 1, 2, 3, 4),
    )


def attend_near_body(io, place, q, k, vt, ids_col, ids_row, p_out, m0, m1):
    attend_quarters(io, (0, 1), place, q, k, vt, ids_col, ids_row, p_out, (m0, m1))


def attend_near(place, q, k, vt, ids_col, ids_row, after=()):
    rows, cols = q.shape
    heads = cols // HEAD
    return call(
        attend_near_body,
        [((2, rows // 4 // MOST, 3 * MOST, heads * MOST), BF)] + [((rows // 4, cols), BF)] * 2,
        [SMEM] + [VMEM] * 5,
        "attend_near",
        (place, q, k, vt, ids_col, ids_row),
        after,
        late=(0,),
    )


def attend_pull(b, q, k, kt, v, p_low, grad):
    heads = q.shape[1] // HEAD
    scale = jnp.asarray(HEAD**-0.5, BF)
    first = pl.multiple_of(b * MOST, MOST)
    span = pl.ds(first, 3 * MOST)
    g_stack = stack_heads(grad, heads)
    q_stack = stack_heads(q[pl.ds(first, MOST), :] * scale, heads)
    weights = p_low.astype(F32)
    grad_probs = nt(v[span, :], g_stack)
    inner = jnp.sum(weights * grad_probs, 0, keepdims=True)
    grad_scores = (weights * (grad_probs - inner)).astype(BF)
    dq = pick_heads(nn(kt[:, span], grad_scores), heads) * (HEAD**-0.5)
    return dq, nn(grad_scores, q_stack), nn(p_low, g_stack)


def rims(place, first, second):
    flip = (place >> 1) != 0
    ends = []
    for here in (slice(0, MOST), slice(-MOST, None)):
        ends.append([jnp.stack([a[here] for a in side[1:]]) for side in (first, second)])
    low = jnp.where(flip, ends[0][1], ends[0][0]).astype(BF)
    high = jnp.where(flip, ends[1][0], ends[1][1]).astype(BF)
    return low, high


def attend_back_body(rels, io, place, q, k, kt, v, probs, ga, gb, dq_out, dk_out, dv_out):
    quarter = ga.shape[0]
    per = quarter // MOST
    base = ((place[0] ^ rels[0]) >> 1) * (2 * per)
    dk_out[...] = jnp.zeros_like(dk_out)
    dv_out[...] = jnp.zeros_like(dv_out)
    for n, (rel, ref) in enumerate(zip(rels, (ga, gb))):
        io.arrive(5, n)

        @pl.loop(0, per, unroll=4)
        def _(i):
            b = (place[0] ^ rel) * per + i
            rows = pl.ds(pl.multiple_of(i * MOST, MOST), MOST)
            dq, dk, dv = attend_pull(b, q, k, kt, v, probs[n, i], ref[rows, :])
            dq_out[n, rows, :] = dq.astype(BF)
            span = pl.ds(pl.multiple_of((b - base) * MOST, MOST), 3 * MOST)
            dk_out[span, :] += dk
            dv_out[span, :] += dv


def attend_back(rels, place, q, k, kt, v, probs, grads, after=(), through=()):
    rows, cols = q.shape
    half = rows // 2 + 2 * MOST
    return call(
        functools.partial(attend_back_body, rels),
        [((2, rows // 4, cols), BF), ((half, cols), F32), ((half, cols), F32)],
        [SMEM] + [VMEM] * 7,
        "attend_back",
        (place, q, k, kt, v, probs, *grads),
        after,
        through,
        lazy=(5,),
    )


def qkv_grads_body(
    io, place, tokens, dqa, dqb, dka, dkb, dva, dvb, from_low, from_high, send_out, keep_out, kv, sums, dwt
):
    rows = tokens.shape[0]
    cols = kv.shape[2]
    quarter, half = rows // 4, rows // 2
    sums[...] = jnp.zeros_like(sums)
    for side, refs in enumerate(((dka, dva), (dkb, dvb))):
        here = pl.ds(pl.multiple_of(((place[0] >> 1) ^ side) * half, half), half + 2 * MOST)
        for j, ref in enumerate(refs):
            sums[j, here, :] += ref[...]
    for j in range(2):
        sums[j, MOST : 2 * MOST, :] += from_low[j].astype(F32)
        sums[j, rows : rows + MOST, :] += from_high[j].astype(F32)
        kv[j] = sums[j, MOST : rows + MOST, :].astype(BF)
    part = 0
    for rel, d in enumerate((dqa.at[0], dqa.at[1], dqb.at[0], dqb.at[1])):
        here = pl.ds(pl.multiple_of((place[0] ^ rel) * quarter, quarter), quarter)
        part = part + tn(d[...], tokens[here, :])
    dwt[0:cols, :] = part
    dwt[cols : 2 * cols, :] = tn(kv[0], tokens[...])
    dwt[2 * cols : 3 * cols, :] = tn(kv[1], tokens[...])
    dwt[3 * cols :, :] = jnp.zeros_like(dwt[3 * cols :, :])
    totals = [col_sum(d[n].astype(F32)) for d in (dqa, dqb) for n in range(2)]
    dwt[3 * cols : 3 * cols + 1, 0:cols] = sum(totals)
    dwt[3 * cols + 1 : 3 * cols + 2, 0:cols] = col_sum(kv[1].astype(F32))
    size = keep_out.shape[0]
    bit = place[1] & 1
    keep_out[...] = dwt[pl.ds(pl.multiple_of(bit * size, size), size), :]
    send_out[...] = dwt[pl.ds(pl.multiple_of((1 - bit) * size, size), size), :].astype(BF)


def qkv_grads(place, tokens, firsts, seconds, from_low, from_high, after=(), through=()):
    (rows, width), cols = tokens.shape, from_low.shape[2]
    pairs = [a for pair in zip(firsts, seconds) for a in pair]
    size = (3 * cols + PAD) // 2
    return call(
        qkv_grads_body,
        [((size, width), BF), ((size, width), F32), ((2, rows, cols), BF)],
        [SMEM] + [VMEM] * 9,
        "qkv_grads",
        (place, tokens, *pairs, from_low, from_high),
        after,
        through,
        scratch=[
            pltpu.VMEM((2, rows + 2 * MOST, cols), F32),
            pltpu.VMEM((3 * cols + PAD, width), F32),
        ],
    )


def input_back_body(io, place, dqa, dqb, kv, wt, *outs):
    quarter = kv.shape[1] // 4
    dq = [dqa.at[0], dqa.at[1], dqb.at[0], dqb.at[1]]
    for rel in (1, 3, 0, 2):
        here = pl.ds(pl.multiple_of((place[0] ^ rel) * quarter, quarter), quarter)
        part = nn(dq[rel][...], wt[0]) + nn(kv[0, here, :], wt[1]) + nn(kv[1, here, :], wt[2])
        outs[rel][...] = part.astype(outs[rel].dtype)


def input_back(place, dqa, dqb, kv, wt, after=(), through=()):
    rows, width = kv.shape[1], wt.shape[2]
    return call(
        input_back_body,
        [((rows // 4, width), BF if rel % 2 else F32) for rel in range(4)],
        [SMEM] + [VMEM] * 4,
        "input_back",
        (place, dqa, dqb, kv, wt),
        after,
        through,
    )


def gelu_parts(pre):
    size = jnp.abs(pre) * (0.5**0.5)
    bell = jnp.exp(-size * size)
    t = 1.0 / (1.0 + 0.3275911 * size)
    poly = 1.061405429
    for c in (-1.453152027, 1.421413741, -0.284496736, 0.254829592):
        poly = poly * t + c
    tail = 0.5 * poly * t * bell
    cdf = jnp.where(pre >= 0, 1.0 - tail, tail)
    return pre * cdf, cdf + pre * bell * 0.3989422804014327


def norm_stats(resid):
    centred = resid - jnp.mean(resid, -1, keepdims=True)
    inv = lax.rsqrt(jnp.mean(centred * centred, -1, keepdims=True) + EPS)
    return centred * inv, inv


def norm_pull(grad, normed, inv, gain):
    scaled = grad * gain
    return inv * (
        scaled
        - jnp.mean(scaled, -1, keepdims=True)
        - normed * jnp.mean(scaled * normed, -1, keepdims=True)
    )


def col_sum(values):
    return jnp.sum(values, 0, keepdims=True)


STEP = 256
PAD = 64
OUT_BIAS, GAIN1, SHIFT1, DOWN_BIAS, GAIN2, SHIFT2 = range(6)


def forward_body(
    io, place, tokens, m0, m1, m2, m3, o0, o1, o2, o3, u0, u1, u2, u3, rows_in,
    normed_out, inv_out, low_out, act_out, slope_out,
):
    cols = m0.shape[1]
    attn = rows_in[OUT_BIAS : OUT_BIAS + 1, :]
    for rel, (m, o) in enumerate(((m0, o0), (m1, o1), (m2, o2), (m3, o3))):
        io.arrive(2 + rel)
        io.arrive(6 + rel)
        attn = attn + nn(m[...], o[0:cols, :])
    io.arrive(1)
    normed, inv = norm_stats(tokens[...].astype(F32) + attn)
    normed_out[...] = normed
    inv_out[...] = inv
    low_out[...] = (normed * rows_in[GAIN1 : GAIN1 + 1, :] + rows_in[SHIFT1 : SHIFT1 + 1, :]).astype(BF)
    io.leave(0)
    io.leave(2)
    for rel, (u, o) in enumerate(((u0, o0), (u1, o1), (u2, o2), (u3, o3))):
        io.arrive(10 + rel)

        @pl.loop(0, u.shape[1] // STEP, unroll=3)
        def _(j):
            here = pl.ds(pl.multiple_of(j * STEP, STEP), STEP)
            bias = col_sum(o[cols : cols + 16, here].astype(F32))
            act, slope = gelu_parts(nn(low_out[...], u[:, here]) + bias)
            act_out[rel, :, here] = act.astype(BF)
            slope_out[rel, :, here] = slope.astype(BF)

        io.leave(3, rel)
        io.leave(4, rel)


def forward(place, tokens, mixed, outs, ups, rows_in, after=()):
    rows, width = tokens.shape[0] // 4, tokens.shape[1]
    hidden = ups[0].shape[1]
    return call(
        forward_body,
        [
            ((rows, width), F32),
            ((rows, 1), F32),
            ((rows, width), BF),
            ((4, rows, hidden), BF),
            ((4, rows, hidden), BF),
        ],
        [SMEM] + [VMEM] * 14,
        "forward",
        (place, tokens, *mixed, *outs, *ups, rows_in),
        after,
        lazy={1: rows, **{i: None for i in range(2, 14)}},
        late=(0, 2, 3, 4),
    )


def middle_body(
    io, place, normed1, act, w0, w1, w2, w3, cot, rows_in,
    result_out, res2_out, low_out, d0, d1, d2, d3, sums_out,
):
    down = rows_in[DOWN_BIAS : DOWN_BIAS + 1, :]
    for rel, w in enumerate((w0, w1, w2, w3)):
        io.arrive(2, rel)
        io.arrive(3 + rel)
        down = down + nn(act[rel], w[...])
    io.arrive(1)
    first = normed1[...] * rows_in[GAIN1 : GAIN1 + 1, :] + rows_in[SHIFT1 : SHIFT1 + 1, :]
    gain2 = rows_in[GAIN2 : GAIN2 + 1, :]
    normed, inv = norm_stats(first + down)
    result_out[...] = (normed * gain2 + rows_in[SHIFT2 : SHIFT2 + 1, :]).astype(BF)
    io.leave(0)
    io.arrive(7)
    grad = cot[...].astype(F32)
    res2 = norm_pull(grad, normed, inv, gain2)
    res2_out[...] = res2
    io.leave(1)
    low = res2.astype(BF)
    low_out[...] = low
    io.leave(2)
    sums_out[0:1, :] = col_sum(grad * normed)
    sums_out[1:2, :] = col_sum(grad)
    sums_out[2:3, :] = col_sum(low.astype(F32))
    for rel in (1, 3, 0, 2):
        (d0, d1, d2, d3)[rel][...] = tn(act[rel], low_out[...]).astype(BF)
        io.leave(3 + rel)


def middle(place, normed1, act, downs, cot, rows_in, after=()):
    rows, width = normed1.shape
    hidden = act.shape[2]
    return call(
        middle_body,
        [
            ((rows, width), BF),
            ((rows, width), F32),
            ((rows, width), BF),
        ]
        + [((hidden, width), BF)] * 4
        + [((3, width), F32)],
        [SMEM] + [VMEM] * 8,
        "middle",
        (place, normed1, act, *downs, cot, rows_in),
        after,
        lazy={2: None, 3: None, 4: None, 5: None, 6: None, 1: None, 7: rows},
        late=(0, 1, 2, 3, 4, 5, 6),
    )


def backward_body(
    io, low2, res2, normed1, inv1, slope, w0, w1, w2, w3, u0, u1, u2, u3, o0, o1, o2, o3, rows_in,
    gup_out, res1_out, low_out, gm0, gm1, gm2, gm3, sums_out, ups_out, total,
):
    cols = gm0.shape[1]
    for rel, (w, u) in enumerate(((w0, u0), (w1, u1), (w2, u2), (w3, u3))):

        @pl.loop(0, u.shape[1] // STEP, unroll=3)
        def _(j):
            here = pl.ds(pl.multiple_of(j * STEP, STEP), STEP)
            grad_act = nt(low2[...], w[here, :])
            low = (grad_act * slope[rel, :, here].astype(F32)).astype(BF)
            gup_out[rel, :, here] = low
            ups_out[rel : rel + 1, here] = col_sum(low.astype(F32))
        total[...] = (res2 if rel == 0 else total)[...] + nt(gup_out[rel], u[...])
    grad = total[...]
    res1 = norm_pull(grad, normed1[...], inv1[...], rows_in[GAIN1 : GAIN1 + 1, :])
    res1_out[...] = res1
    low = res1.astype(BF)
    low_out[...] = low
    sums_out[0:1, :] = col_sum(grad * normed1[...])
    sums_out[1:2, :] = col_sum(grad)
    sums_out[2:3, :] = col_sum(low.astype(F32))
    for rel, (gm_out, o) in enumerate(zip((gm0, gm1, gm2, gm3), (o0, o1, o2, o3))):
        gm_out[...] = nt(low, o[0:cols, :]).astype(BF)


def backward(low2, res2, normed1, inv1, slope, downs, ups, outs, rows_in, cols, after=()):
    rows, width = low2.shape
    hidden = slope.shape[2]
    return call(
        backward_body,
        [
            ((4, rows, hidden), BF),
            ((rows, width), F32),
            ((rows, width), BF),
        ]
        + [((rows, cols), BF)] * 4
        + [
            ((3, width), F32),
            ((4, hidden), F32),
        ],
        [VMEM] * 18,
        "backward",
        (low2, res2, normed1, inv1, slope, *downs, *ups, *outs, rows_in),
        after,
        scratch=[pltpu.VMEM((rows, width), F32)],
    )


def up_grads_body(io, low1, gup, *outs):
    for rel in (1, 3, 0, 2):
        outs[rel][...] = tn(low1[:, 0 : outs[rel].shape[0]], gup[rel]).astype(BF)


def up_grads(low1, gup, first, after=()):
    return call(
        up_grads_body,
        [((first, gup.shape[2]), BF)] * 4,
        [VMEM] * 2,
        "up_grads",
        (low1, gup),
        after,
    )


def out_grads_body(io, low1, gup, grad_low, m0, m1, m2, m3, sums1, sums2, ups, *outs):
    width, cols = low1.shape[1], m0.shape[1]
    left = outs[0].shape[0] - cols - PAD
    mixed = (m0, m1, m2, m3)
    for rel in (1, 3, 0, 2):
        out = outs[rel]
        out[0:left, :] = tn(low1[:, width - left :], gup[rel]).astype(BF)
        out[left : left + cols, :] = tn(mixed[rel][...], grad_low[...]).astype(BF)
        rows = jnp.concatenate([sums2[...], sums1[...], ups[rel : rel + 1, :]], 0)
        rows = jnp.concatenate([rows, jnp.zeros((PAD - rows.shape[0], width), F32)], 0)
        out[left + cols :, :] = rows.astype(BF)


def out_grads(low1, gup, grad_low, mixed, sums1, sums2, ups, left, after=()):
    hidden = gup.shape[2]
    cols = mixed[0].shape[1]
    return call(
        out_grads_body,
        [((left + cols + PAD, hidden), BF)] * 4,
        [VMEM] * 10,
        "out_grads",
        (low1, gup, grad_low, *mixed, sums1, sums2, ups),
        after,
    )


def place_rows_body(io, place, p0, p1, p2, p3, out):
    quarter = p0.shape[0]
    for rel, p in enumerate((p0, p1, p2, p3)):
        here = pl.ds(pl.multiple_of((place[0] ^ rel) * quarter, quarter), quarter)
        out[here, :] = p[...].astype(out.dtype)


def place_rows(place, parts, dtype, after=()):
    quarter, width = parts[0].shape
    return call(
        place_rows_body,
        [((4 * quarter, width), dtype)],
        [SMEM] + [VMEM] * 4,
        "place_low" if dtype == BF else "place_rows",
        (place, *parts),
        after,
    )[0]


def swap(value, axis, bits):
    count = lax.axis_size(axis)
    return lax.ppermute(value, axis, [(i, i ^ bits) for i in range(count)])


def gather_rel(own):
    far = swap(own, "tp", 2)
    return (own, swap(own, "tp", 1), far, swap(far, "tp", 1))


def core_swap(parts):
    return parts[0], swap(parts[1], "tp", 1), parts[2], swap(parts[3], "tp", 1)


def core_sum(keep, got, keep_far, got_far):
    return total(keep, got).astype(BF), total(keep_far, got_far).astype(BF)


def total(keep, got):
    return keep.astype(F32) + got.astype(F32)


def divide(part, level):
    return divide_sum((part,), level)


def divide_sum(parts, level):
    half = parts[0].shape[0] // 2
    first = ((lax.axis_index("seq") >> level) & 1) * half
    send = sum(lax.dynamic_slice_in_dim(p, half - first, half, 0).astype(F32) for p in parts)
    keep = sum(lax.dynamic_slice_in_dim(p, first, half, 0).astype(F32) for p in parts)
    return send.astype(BF), keep


def join(part, other, level):
    upper = ((lax.axis_index("seq") >> level) & 1) != 0
    return jnp.where(
        upper, jnp.concatenate([other, part], 0), jnp.concatenate([part, other], 0)
    )


class Line:
    def __init__(self, first):
        self.last = first

    def take(self, *arrays):
        *arrays, _ = lax.optimization_barrier((*arrays, self.last))
        return arrays if len(arrays) > 1 else arrays[0]

    def put(self, *arrays):
        self.last = arrays[0]
        return arrays if len(arrays) > 1 else arrays[0]


class SeqSum:
    def __init__(self, line, bits):
        self.line, self.bits = line, bits

    def first(self, own, far=None):
        parts = [self.line.take(own)] if far is None else self.line.take(own, far)
        send, self.keep = self.line.put(*divide_sum(parts, self.bits[0]))
        self.got = swap(send, "seq", 1 << self.bits[0])

    def second(self):
        parts = self.line.take(self.keep, self.got)
        send, self.keep = self.line.put(*divide_sum(parts, self.bits[1]))
        self.got = swap(send, "seq", 1 << self.bits[1])

    def third(self):
        part = self.line.put(total(*self.line.take(self.keep, self.got)).astype(BF))
        levels = lax.axis_size("seq").bit_length() - 1
        for k in range(2, levels - 1):
            part = total(part, swap(part, "seq", 1 << k)).astype(BF)
        self.keep, self.got = part, swap(part, "seq", 1 << (levels - 1))

    def fourth(self):
        self.keep = self.line.put(total(*self.line.take(self.keep, self.got)).astype(BF))
        self.got = swap(self.keep, "seq", 1 << self.bits[1])

    def fifth(self):
        self.keep = self.line.put(join(*self.line.take(self.keep, self.got), self.bits[1]))
        self.got = swap(self.keep, "seq", 1 << self.bits[0])

    def sixth(self):
        part, other = self.line.take(self.keep, self.got)
        upper = ((lax.axis_index("seq") >> self.bits[0]) & 1) != 0
        return jnp.where(upper, other, part).astype(F32), jnp.where(upper, part, other).astype(F32)


def on_device(
    tokens, cotangent, lengths, w_qkv, qv_bias, w_out, out_bias, gain_first, shift_first,
    w_up, up_bias, w_down, down_bias, gain_second, shift_second,
):
    rows, width = tokens.shape
    quarter = rows // 4
    cols = w_qkv.shape[2]
    hidden = w_up.shape[1]
    seq_count = lax.axis_size("seq")
    tp_place = lax.axis_index("tp")
    seq_place = lax.axis_index("seq")
    place = jnp.stack([tp_place, seq_place, rows * seq_count]).astype(jnp.int32)
    forwards = [(i, i + 1) for i in range(seq_count - 1)]
    backwards = [(b, a) for a, b in forwards]

    vectors = [out_bias, gain_first, shift_first, down_bias, gain_second, shift_second]
    high, low, bundle, half_d, rows_in = prepare(
        place, tokens, w_out, w_up, w_down, up_bias, vectors
    )
    low, high = lax.ppermute(high, "seq", forwards), lax.ppermute(low, "seq", backwards)
    own_o = bundle[: cols + 16]
    bundle, half_d = swap(bundle, "tp", 2), swap(half_d, "tp", 2)
    wt = jnp.transpose(w_qkv, (0, 2, 1))
    q, k, v, kt, vt, ids_col, ids_row = project(
        place, tokens, wt, qv_bias, lengths.reshape(1, -1), (rows_in,)
    )
    own_o, own_u, own_d, _ = lax.optimization_barrier((own_o, w_up, w_down, q))
    near_o, near_u, near_d = [swap(a, "tp", 1) for a in (own_o, own_u, own_d)]
    p_far, k, v, kt, vt, mixed2, mixed3 = attend_far(
        place, q, k, v, kt, vt, ids_col, ids_row, low, high, wt, qv_bias
    )
    mixed2, mixed3 = swap(mixed2, "tp", 2), swap(mixed3, "tp", 3)
    line = Line(p_far)
    bundle = line.take(bundle)
    far_o, half_u = line.put(bundle[: cols + 16], bundle[cols + 16 :])
    other_u = swap(half_u, "seq", 1)
    last_o = swap(far_o, "tp", 1)
    p_near, mixed0, mixed1 = attend_near(place, q, k, vt, ids_col, ids_row, (line.last,))
    line.put(p_near)
    half_d = line.put(line.take(half_d))
    other_d = swap(half_d, "seq", 1)
    mixed = [mixed0, swap(mixed1, "tp", 1), mixed2, mixed3]
    mixed = line.put(*line.take(*mixed))
    far_u = line.put(join(*line.take(half_u, other_u), 0))
    last_u = swap(far_u, "tp", 1)
    outs, ups = (own_o, near_o, far_o, last_o), (own_u, near_u, far_u, last_u)
    normed1, inv1, low1, act, slope = forward(place, tokens, mixed, outs, ups, rows_in)
    line.put(normed1)
    far_d = line.put(join(*line.take(half_d, other_d), 0))
    downs = (own_d, near_d, far_d, swap(far_d, "tp", 1))
    result, res2, low2, *parts_d, sums2 = middle(
        place, normed1, act, downs, cotangent, rows_in
    )
    act_far, act_near = swap(result, "tp", 2), swap(result, "tp", 1)
    parts_d = core_swap(parts_d)
    gup, res1, grad_low, g0, g1, g2, g3, sums1, up_sums = backward(
        low2, res2, normed1, inv1, slope, downs, ups, outs, rows_in, cols
    )
    g1, g2, g3 = swap(g1, "tp", 1), swap(g2, "tp", 2), swap(g3, "tp", 3)
    own_d, far_d = core_sum(*parts_d)
    left = width - 512
    parts_u = up_grads(low1, gup, width - left, (own_d, far_d, act_far, act_near, g1))
    parts_v = out_grads(
        low1, gup, grad_low, mixed, sums1, sums2, up_sums, left, (parts_u[0],)
    )
    line = Line(parts_v[0])
    sum_d, sum_q, sum_u, sum_v = [
        SeqSum(line, bits) for bits in ((0, 1), (0, 1), (1, 0), (1, 0))
    ]
    firsts = attend_back((0, 1), place, q, k, kt, v, p_near, (g0, g1), (line.last,))
    line.put(firsts[0])
    sum_d.first(own_d, swap(far_d, "tp", 2))
    own_u, far_u = line.put(*core_sum(*line.take(*core_swap(parts_u))))
    *seconds, sum_d.keep = attend_back(
        (2, 3), place, q, k, kt, v, p_far, (g2, g3), (line.last,), (sum_d.keep,)
    )
    line.put(seconds[0])
    low_rim, high_rim = line.put(*rims(tp_place, firsts, seconds))
    from_high = lax.ppermute(low_rim, "seq", backwards)
    from_low = lax.ppermute(high_rim, "seq", forwards)
    own_v, far_v = line.put(*core_sum(*line.take(*core_swap(parts_v))))
    sum_d.second()
    sum_u.first(own_u, swap(far_u, "tp", 2))
    send_q, sum_q.keep, kv, sum_d.keep, sum_u.keep = qkv_grads(
        place, tokens, firsts, seconds, from_low, from_high, (line.last,),
        (sum_d.keep, sum_u.keep),
    )
    sum_q.got = swap(send_q, "seq", 1)
    line.put(send_q)
    sum_d.third()
    sum_u.second()
    act_last = swap(act_far, "tp", 1)
    *parts_i, sum_u.keep, sum_q.keep, own_v = input_back(
        place, firsts[0], seconds[0], kv, wt, (line.last, act_last),
        (sum_u.keep, sum_q.keep, own_v),
    )
    line.put(parts_i[0])
    parts_i = core_swap(parts_i)
    sum_v.first(own_v, swap(far_v, "tp", 2))
    sum_q.second()
    sum_u.third()
    result = place_rows(place, line.take(result, act_near, act_far, act_last), BF)
    line.put(result)
    *parts_i, keep_far, got_far = line.take(*parts_i)
    far_i = swap(line.put(total(keep_far, got_far).astype(BF)), "tp", 2)
    sum_v.second()
    sum_d.fourth()
    sum_q.third()
    sum_u.fourth()
    sum_v.third()
    sum_d.fifth()
    far_i = line.take(far_i)
    part = line.put((total(*parts_i) + far_i.astype(F32) + res1).astype(BF))
    part_far, part_near = swap(part, "tp", 2), swap(part, "tp", 1)
    sum_q.fourth()
    sum_u.fifth()
    sum_v.fourth()
    sum_q.fifth()
    grad_down = line.put(jnp.concatenate(sum_d.sixth(), 0))
    sum_v.fifth()
    part_far = line.put(line.take(part_far))
    part_last = swap(part_far, "tp", 1)
    input_grad = place_rows(place, line.take(part, part_near, part_far, part_last), F32)
    line.put(input_grad)
    lower, upper = sum_q.sixth()
    grad_qkv = line.put(jnp.concatenate([lower, upper[: -PAD]], 0))
    qv_sums = upper[-PAD : 2 - PAD, :cols]
    grad_qkv = jnp.transpose(grad_qkv.reshape(3, cols, width), (0, 2, 1))
    lower, upper = sum_v.sixth()
    grad_up = jnp.concatenate([*sum_u.sixth(), lower, upper[: left - lower.shape[0]]], 0)
    grad_rest = upper[left - lower.shape[0] :]
    grad_out = grad_rest[:cols]
    sums = grad_rest[cols:]
    return (
        result, input_grad, grad_qkv, qv_sums, grad_out, sums[5], sums[3], sums[4],
        grad_up, sums[6], grad_down, sums[2], sums[0], sums[1],
    )


def solution(mesh):
    rep, rows = P(), P("seq", None)
    return jax.shard_map(
        on_device,
        mesh=mesh,
        in_specs=(
            rows, rows, rep, P(None, None, "tp"), P(None, "tp"), P("tp", None), rep, rep, rep,
            P(None, "tp"), P("tp"), P("tp", None), rep, rep, rep,
        ),
        out_specs=(
            rows, rows, P(None, None, "tp"), P(None, "tp"), P("tp", None), rep, rep, rep,
            P(None, "tp"), P("tp"), P("tp", None), rep, rep, rep,
        ),
        check_vma=False,
    )
```

```python
import functools
import types

import jax
import jax.numpy as jnp
from jax import lax
from jax.experimental import pallas as pl
from jax.experimental.pallas import tpu as pltpu
from jax.sharding import PartitionSpec as P

HEAD = 64
MOST = 128
EPS = 1e-12
BF = jnp.bfloat16
F32 = jnp.float32
MIB = 1024 * 1024


def nn(left, right):
    return lax.dot_general(left, right, (((1,), (0,)), ((), ())), preferred_element_type=F32)


def nt(left, right):
    return lax.dot_general(left, right, (((1,), (1,)), ((), ())), preferred_element_type=F32)


def tn(left, right):
    return lax.dot_general(left, right, (((0,), (0,)), ((), ())), preferred_element_type=F32)


VMEM = pl.BlockSpec(memory_space=pltpu.VMEM)
SMEM = pl.BlockSpec(memory_space=pltpu.SMEM)


COST = {
    "prepare": 2, "project": 3, "attend_far": 3, "attend_near": 3, "forward": 6, "middle": 5, "backward": 6, "place_rows": 2, "up_grads": 0.5, "out_grads": 0.5, "attend_back": 1, "qkv_grads": 1, "input_back": 3, "place_low": 4,
}
ANY = pl.BlockSpec(memory_space=pl.ANY)


def call(
    body, outs, specs, name, args, after=(), through=(), scratch=(), limit=56, lazy=(), late=(), raw=()
):
    given, extra, made = len(args), len(after) + len(through), len(outs)
    rows_of = dict(lazy) if isinstance(lazy, dict) else {i: None for i in lazy}
    specs = [ANY if i in rows_of else spec for i, spec in enumerate(specs)]

    def split_of(shape):
        return shape[0] if len(shape) > 2 and shape[0] in (2, 4) else 1

    buffers, sems = [], []
    for i, rows in rows_of.items():
        shape = args[i].shape if rows is None else (rows,) + args[i].shape[1:]
        buffers.append(pltpu.VMEM(shape, args[i].dtype))
        sems.append(pltpu.SemaphoreType.DMA((split_of(shape),)))
    for o in late:
        shape, dtype = outs[o]
        buffers.append(pltpu.VMEM(shape, dtype))
        sems.append(pltpu.SemaphoreType.DMA((split_of(shape),)))
    staged = len(buffers)

    def whole(*refs):
        ins, results = list(refs[:given]), list(refs[given + extra : given + extra + made])
        rest = refs[given + extra + made + len(through) :]
        held, marks, rest = rest[:staged], rest[staged : 2 * staged], rest[2 * staged :]
        coming, going, left = {}, {}, []

        def copies(source, target, mark):
            count = split_of(target.shape)
            if count == 1:
                return [pltpu.make_async_copy(source, target, mark.at[0])]
            return [
                pltpu.make_async_copy(source.at[p], target.at[p], mark.at[p]) for p in range(count)
            ]

        for (i, rows), buffer, mark in zip(rows_of.items(), held, marks):
            source = ins[i]
            if rows is not None:
                source = source.at[pl.ds(pl.multiple_of(ins[0][0] * rows, rows), rows)]
            coming[i] = copies(source, buffer, mark)
            ins[i] = buffer
        for o, buffer, mark in zip(late, held[len(rows_of) :], marks[len(rows_of) :]):
            going[o] = copies(buffer, results[o], mark)
            results[o] = buffer
        for group in coming.values():
            for copy in group:
                copy.start()

        def arrive(i, p=0):
            coming[i][p].wait()

        def leave(o, p=0):
            going[o][p].start()
            left.append(going[o][p])

        body(types.SimpleNamespace(arrive=arrive, leave=leave), *ins, *results, *rest)
        for copy in left:
            copy.wait()

    return pl.pallas_call(
        whole,
        out_shape=[jax.ShapeDtypeStruct(shape, dtype) for shape, dtype in outs]
        + [jax.ShapeDtypeStruct(a.shape, a.dtype) for a in through],
        in_specs=list(specs) + [ANY] * extra,
        out_specs=[ANY if o in late or o in raw else VMEM for o in range(made)] + [ANY] * len(through),
        scratch_shapes=buffers + sems + list(scratch),
        name=name,
        input_output_aliases={given + len(after) + n: made + n for n in range(len(through))},
        cost_estimate=pl.CostEstimate(
            flops=int(COST.get(name, 2) * 1_000_000_000), bytes_accessed=0, transcendentals=0
        ),
        compiler_params=pltpu.CompilerParams(vmem_limit_bytes=limit * MIB),
    )(*args, *after, *through)


def stack_heads(block, heads):
    lane = lax.broadcasted_iota(jnp.int32, block.shape, 1) // HEAD
    zero = jnp.zeros_like(block)
    return jnp.concatenate([jnp.where(lane == h, block, zero) for h in range(heads)], 0)


def pick_heads(stacked, heads):
    size = stacked.shape[1] // heads
    rows = [stacked[h * HEAD : (h + 1) * HEAD, h * size : (h + 1) * size] for h in range(heads)]
    return jnp.concatenate(rows, 0).T


def prepare_body(
    io, place, tokens, w_out, w_up, w_down, up_bias, b0, b1, b2, b3, b4, b5,
    high_out, low_out, own_out, half_down, rows_out, marks,
):
    rows, cols = tokens.shape[0], w_out.shape[0]
    half = half_down.shape[0]
    mine = pl.ds(pl.multiple_of((place[1] & 1) * half, half), half)
    copies = [
        pltpu.make_async_copy(source, target, marks.at[n])
        for n, (source, target) in enumerate(
            (
                (tokens.at[pl.ds(rows - MOST, MOST)], high_out),
                (tokens.at[pl.ds(0, MOST)], low_out),
                (w_out, own_out.at[pl.ds(0, cols)]),
                (w_up.at[mine], own_out.at[pl.ds(cols + 16, half)]),
                (w_down.at[mine], half_down),
            )
        )
    ]
    for copy in copies:
        copy.start()
    rest = up_bias[...].reshape(1, -1)
    pieces = []
    for _ in range(3):
        pieces.append(rest.astype(BF).astype(F32))
        rest = rest - pieces[-1]
    pieces = jnp.concatenate(pieces + [jnp.zeros((13, rest.shape[1]), F32)], 0)
    own_out[cols : cols + 16, :] = pieces.astype(BF)
    rows_out[...] = jnp.zeros_like(rows_out)
    for n, ref in enumerate((b0, b1, b2, b3, b4, b5)):
        rows_out[n : n + 1, :] = ref[...].reshape(1, -1)
    for copy in copies:
        copy.wait()


def prepare(place, tokens, w_out, w_up, w_down, up_bias, vectors):
    width = tokens.shape[1]
    half = (w_up.shape[0] // 2, width)
    return call(
        prepare_body,
        [((MOST, width), BF)] * 2
        + [((w_out.shape[0] + 16 + half[0], width), BF), (half, BF), ((8, width), F32)],
        [SMEM] + [ANY] * 4 + [VMEM] * 7,
        "prepare",
        (place, tokens, w_out, w_up, w_down, up_bias, *vectors),
        scratch=[pltpu.SemaphoreType.DMA((5,))],
    )


def project_block(block, wt, bias, target, k_out, v_out, kt_out, vt_out):
    span = pl.ds(target, block.shape[0])
    keys = nt(block, wt[1])
    k_out[span, :] = keys.astype(BF)
    kt_out[:, span] = keys.T.astype(BF)
    values = nt(block, wt[2]) + bias[1:2, :]
    v_out[span, :] = values.astype(BF)
    vt_out[:, span] = values.T.astype(BF)


def project_body(
    io, place, tokens, wt, bias, lengths, q_out, k_out, v_out, kt_out, vt_out, col_out, row_out
):
    rows = tokens.shape[0]
    ext = col_out.shape[0]
    sents = lengths.shape[1]
    step = 256

    lens = jnp.broadcast_to(lengths[...], (sents, sents))
    down = lax.broadcasted_iota(jnp.int32, (sents, sents), 0)
    across = lax.broadcasted_iota(jnp.int32, (sents, sents), 1)
    ends_col = jnp.sum(jnp.where(across <= down, lens, 0), 1, keepdims=True)
    ends_row = jnp.sum(jnp.where(down == across, ends_col, 0), 0, keepdims=True)
    first = place[1] * rows - MOST

    def sentence(at, ends, axis):
        passed = jnp.sum((ends <= at).astype(jnp.int32), axis, keepdims=True)
        return jnp.where((at < 0) | (at >= place[2]), -1, passed)

    @pl.loop(0, ext // step, unroll=3)
    def _(i):
        base = pl.multiple_of(i * step, step)
        at = first + base
        row_out[:, pl.ds(base, step)] = sentence(
            at + lax.broadcasted_iota(jnp.int32, (1, step), 1), ends_col, 0
        )
        col_out[pl.ds(base, step), :] = sentence(
            at + lax.broadcasted_iota(jnp.int32, (step, 1), 0), ends_row, 1
        )

    io.arrive(1)

    @pl.loop(0, rows // step, unroll=4)
    def _(i):
        first = pl.multiple_of(i * step, step)
        block = tokens[pl.ds(first, step), :]
        q_out[pl.ds(first, step), :] = (nt(block, wt[0]) + bias[0:1, :]).astype(BF)
        target = pl.multiple_of(first + MOST, MOST)
        project_block(block, wt, bias, target, k_out, v_out, kt_out, vt_out)


def project(place, tokens, wt, bias, lengths, after=()):
    rows, cols = tokens.shape[0], wt.shape[1]
    ext = rows + 2 * MOST
    return call(
        project_body,
        [((rows, cols), BF), ((ext, cols), BF), ((ext, cols), BF), ((cols, ext), BF), ((cols, ext), BF)]
        + [((ext, 1), jnp.int32), ((1, ext), jnp.int32)],
        [SMEM] + [VMEM] * 4,
        "project",
        (place, tokens, wt, bias, lengths),
        after,
        lazy=(1,),
    )


def attend_quarters(io, rels, place, q, k, vt, ids_col, ids_row, p_out, mixed_outs):
    rows, cols = q.shape
    heads = cols // HEAD
    scale = jnp.asarray(HEAD**-0.5, BF)
    per = rows // 4 // MOST
    for n, (rel, mixed_out) in enumerate(zip(rels, mixed_outs)):

        @pl.loop(0, per, unroll=4)
        def _(i):
            b = (place[0] ^ rel) * per + i
            first = pl.multiple_of(b * MOST, MOST)
            span = pl.ds(first, 3 * MOST)
            q3 = stack_heads(q[pl.ds(first, MOST), :] * scale, heads)
            scores = nt(k[span, :], q3)
            mine = ids_row[:, pl.ds(pl.multiple_of(first + MOST, MOST), MOST)]
            mask = ids_col[span, :] == mine
            scores = jnp.where(jnp.concatenate([mask] * heads, 1), scores, -1e30)
            raised = jnp.exp(scores - jnp.max(scores, 0, keepdims=True))
            probs = raised * (1.0 / jnp.sum(raised, 0, keepdims=True))
            probs = probs.astype(BF)
            p_out[n, i] = probs
            mixed = pick_heads(nn(vt[:, span], probs), heads)
            mixed_out[pl.ds(pl.multiple_of(i * MOST, MOST), MOST), :] = mixed.astype(BF)

        io.leave(0, n)


def attend_far_body(
    io, place, q, k_in, v_in, kt_in, vt_in, ids_col, ids_row, low, high, wt, bias,
    p_out, k_out, v_out, kt_out, vt_out, m0, m1, marks,
):
    rows = q.shape[0]
    held = (k_out, v_out, kt_out, vt_out)
    copies = [
        pltpu.make_async_copy(source, target, marks.at[n])
        for n, (source, target) in enumerate(zip((k_in, v_in, kt_in, vt_in), held))
    ]
    for copy in copies:
        copy.start()
    for copy in copies:
        copy.wait()
    project_block(low[...], wt, bias, 0, *held)
    project_block(high[...], wt, bias, rows + MOST, *held)
    for o in (1, 2, 3, 4):
        io.leave(o)
    attend_quarters(io, (2, 3), place, q, k_out, vt_out, ids_col, ids_row, p_out, (m0, m1))


def attend_far(place, q, k, v, kt, vt, ids_col, ids_row, low, high, wt, bias, after=()):
    rows, cols = q.shape
    heads = cols // HEAD
    return call(
        attend_far_body,
        [((2, rows // 4 // MOST, 3 * MOST, heads * MOST), BF)]
        + [(a.shape, BF) for a in (k, v, kt, vt)]
        + [((rows // 4, cols), BF)] * 2,
        [SMEM, VMEM] + [ANY] * 4 + [VMEM] * 6,
        "attend_far",
        (place, q, k, v, kt, vt, ids_col, ids_row, low, high, wt, bias),
        after,
        scratch=[pltpu.SemaphoreType.DMA((4,))],
        late=(0, 1, 2, 3, 4),
    )


def attend_near_body(io, place, q, k, vt, ids_col, ids_row, p_out, m0, m1):
    attend_quarters(io, (0, 1), place, q, k, vt, ids_col, ids_row, p_out, (m0, m1))


def attend_near(place, q, k, vt, ids_col, ids_row, after=()):
    rows, cols = q.shape
    heads = cols // HEAD
    return call(
        attend_near_body,
        [((2, rows // 4 // MOST, 3 * MOST, heads * MOST), BF)] + [((rows // 4, cols), BF)] * 2,
        [SMEM] + [VMEM] * 5,
        "attend_near",
        (place, q, k, vt, ids_col, ids_row),
        after,
        late=(0,),
    )


def attend_pull(b, q, k, kt, v, p_low, grad):
    heads = q.shape[1] // HEAD
    scale = jnp.asarray(HEAD**-0.5, BF)
    first = pl.multiple_of(b * MOST, MOST)
    span = pl.ds(first, 3 * MOST)
    g_stack = stack_heads(grad, heads)
    q_stack = stack_heads(q[pl.ds(first, MOST), :] * scale, heads)
    weights = p_low.astype(F32)
    grad_probs = nt(v[span, :], g_stack)
    inner = jnp.sum(weights * grad_probs, 0, keepdims=True)
    grad_scores = (weights * (grad_probs - inner)).astype(BF)
    dq = pick_heads(nn(kt[:, span], grad_scores), heads) * (HEAD**-0.5)
    return dq, nn(grad_scores, q_stack), nn(p_low, g_stack)


def rims(place, first, second):
    flip = (place >> 1) != 0
    ends = []
    for here in (slice(0, MOST), slice(-MOST, None)):
        ends.append([jnp.stack([a[here] for a in side[1:]]) for side in (first, second)])
    low = jnp.where(flip, ends[0][1], ends[0][0]).astype(BF)
    high = jnp.where(flip, ends[1][0], ends[1][1]).astype(BF)
    return low, high


def attend_back_body(rels, io, place, q, k, kt, v, probs, ga, gb, dq_out, dk_out, dv_out):
    quarter = ga.shape[0]
    per = quarter // MOST
    base = ((place[0] ^ rels[0]) >> 1) * (2 * per)
    dk_out[...] = jnp.zeros_like(dk_out)
    dv_out[...] = jnp.zeros_like(dv_out)
    for n, (rel, ref) in enumerate(zip(rels, (ga, gb))):
        io.arrive(5, n)

        @pl.loop(0, per, unroll=4)
        def _(i):
            b = (place[0] ^ rel) * per + i
            rows = pl.ds(pl.multiple_of(i * MOST, MOST), MOST)
            dq, dk, dv = attend_pull(b, q, k, kt, v, probs[n, i], ref[rows, :])
            dq_out[n, rows, :] = dq.astype(BF)
            span = pl.ds(pl.multiple_of((b - base) * MOST, MOST), 3 * MOST)
            dk_out[span, :] += dk
            dv_out[span, :] += dv


def attend_back(rels, place, q, k, kt, v, probs, grads, after=(), through=()):
    rows, cols = q.shape
    half = rows // 2 + 2 * MOST
    return call(
        functools.partial(attend_back_body, rels),
        [((2, rows // 4, cols), BF), ((half, cols), F32), ((half, cols), F32)],
        [SMEM] + [VMEM] * 7,
        "attend_back",
        (place, q, k, kt, v, probs, *grads),
        after,
        through,
        lazy=(5,),
    )


def qkv_grads_body(
    io, place, tokens, dqa, dqb, dka, dkb, dva, dvb, from_low, from_high, send_out, keep_out, kv, sums, dwt
):
    rows = tokens.shape[0]
    cols = kv.shape[2]
    quarter, half = rows // 4, rows // 2
    sums[...] = jnp.zeros_like(sums)
    for side, refs in enumerate(((dka, dva), (dkb, dvb))):
        here = pl.ds(pl.multiple_of(((place[0] >> 1) ^ side) * half, half), half + 2 * MOST)
        for j, ref in enumerate(refs):
            sums[j, here, :] += ref[...]
    for j in range(2):
        sums[j, MOST : 2 * MOST, :] += from_low[j].astype(F32)
        sums[j, rows : rows + MOST, :] += from_high[j].astype(F32)
        kv[j] = sums[j, MOST : rows + MOST, :].astype(BF)
    part = 0
    for rel, d in enumerate((dqa.at[0], dqa.at[1], dqb.at[0], dqb.at[1])):
        here = pl.ds(pl.multiple_of((place[0] ^ rel) * quarter, quarter), quarter)
        part = part + tn(d[...], tokens[here, :])
    dwt[0:cols, :] = part
    dwt[cols : 2 * cols, :] = tn(kv[0], tokens[...])
    dwt[2 * cols : 3 * cols, :] = tn(kv[1], tokens[...])
    dwt[3 * cols :, :] = jnp.zeros_like(dwt[3 * cols :, :])
    totals = [col_sum(d[n].astype(F32)) for d in (dqa, dqb) for n in range(2)]
    dwt[3 * cols : 3 * cols + 1, 0:cols] = sum(totals)
    dwt[3 * cols + 1 : 3 * cols + 2, 0:cols] = col_sum(kv[1].astype(F32))
    size = keep_out.shape[0]
    bit = place[1] & 1
    keep_out[...] = dwt[pl.ds(pl.multiple_of(bit * size, size), size), :]
    send_out[...] = dwt[pl.ds(pl.multiple_of((1 - bit) * size, size), size), :].astype(BF)


def qkv_grads(place, tokens, firsts, seconds, from_low, from_high, after=(), through=()):
    (rows, width), cols = tokens.shape, from_low.shape[2]
    pairs = [a for pair in zip(firsts, seconds) for a in pair]
    size = (3 * cols + PAD) // 2
    return call(
        qkv_grads_body,
        [((size, width), BF), ((size, width), F32), ((2, rows, cols), BF)],
        [SMEM] + [VMEM] * 9,
        "qkv_grads",
        (place, tokens, *pairs, from_low, from_high),
        after,
        through,
        scratch=[
            pltpu.VMEM((2, rows + 2 * MOST, cols), F32),
            pltpu.VMEM((3 * cols + PAD, width), F32),
        ],
    )


def input_back_body(io, place, dqa, dqb, kv, wt, *outs):
    quarter = kv.shape[1] // 4
    dq = [dqa.at[0], dqa.at[1], dqb.at[0], dqb.at[1]]
    for rel in (1, 3, 0, 2):
        here = pl.ds(pl.multiple_of((place[0] ^ rel) * quarter, quarter), quarter)
        part = nn(dq[rel][...], wt[0]) + nn(kv[0, here, :], wt[1]) + nn(kv[1, here, :], wt[2])
        outs[rel][...] = part.astype(outs[rel].dtype)


def input_back(place, dqa, dqb, kv, wt, after=(), through=()):
    rows, width = kv.shape[1], wt.shape[2]
    return call(
        input_back_body,
        [((rows // 4, width), BF if rel % 2 else F32) for rel in range(4)],
        [SMEM] + [VMEM] * 4,
        "input_back",
        (place, dqa, dqb, kv, wt),
        after,
        through,
    )


def gelu_parts(pre):
    size = jnp.abs(pre) * (0.5**0.5)
    bell = jnp.exp(-size * size)
    t = 1.0 / (1.0 + 0.3275911 * size)
    poly = 1.061405429
    for c in (-1.453152027, 1.421413741, -0.284496736, 0.254829592):
        poly = poly * t + c
    tail = 0.5 * poly * t * bell
    cdf = jnp.where(pre >= 0, 1.0 - tail, tail)
    return pre * cdf, cdf + pre * bell * 0.3989422804014327


def norm_stats(resid):
    centred = resid - jnp.mean(resid, -1, keepdims=True)
    inv = lax.rsqrt(jnp.mean(centred * centred, -1, keepdims=True) + EPS)
    return centred * inv, inv


def norm_pull(grad, normed, inv, gain):
    scaled = grad * gain
    return inv * (
        scaled
        - jnp.mean(scaled, -1, keepdims=True)
        - normed * jnp.mean(scaled * normed, -1, keepdims=True)
    )


def col_sum(values):
    return jnp.sum(values, 0, keepdims=True)


STEP = 256
PAD = 64
OUT_BIAS, GAIN1, SHIFT1, DOWN_BIAS, GAIN2, SHIFT2 = range(6)


def forward_body(
    io, place, tokens, m0, m1, m2, m3, o0, o1, o2, o3, u0, u1, u2, u3, rows_in,
    normed_out, inv_out, low_out, act_out, slope_out,
):
    cols = m0.shape[1]
    attn = rows_in[OUT_BIAS : OUT_BIAS + 1, :]
    for rel, (m, o) in enumerate(((m0, o0), (m1, o1), (m2, o2), (m3, o3))):
        io.arrive(2 + rel)
        io.arrive(6 + rel)
        attn = attn + nn(m[...], o[0:cols, :])
    io.arrive(1)
    normed, inv = norm_stats(tokens[...].astype(F32) + attn)
    normed_out[...] = normed
    inv_out[...] = inv
    low_out[...] = (normed * rows_in[GAIN1 : GAIN1 + 1, :] + rows_in[SHIFT1 : SHIFT1 + 1, :]).astype(BF)
    io.leave(0)
    io.leave(2)
    for rel, (u, o) in enumerate(((u0, o0), (u1, o1), (u2, o2), (u3, o3))):
        io.arrive(10 + rel)

        @pl.loop(0, u.shape[1] // STEP, unroll=3)
        def _(j):
            here = pl.ds(pl.multiple_of(j * STEP, STEP), STEP)
            bias = col_sum(o[cols : cols + 16, here].astype(F32))
            act, slope = gelu_parts(nn(low_out[...], u[:, here]) + bias)
            act_out[rel, :, here] = act.astype(BF)
            slope_out[rel, :, here] = slope.astype(BF)

        io.leave(3, rel)
        io.leave(4, rel)


def forward(place, tokens, mixed, outs, ups, rows_in, after=()):
    rows, width = tokens.shape[0] // 4, tokens.shape[1]
    hidden = ups[0].shape[1]
    return call(
        forward_body,
        [
            ((rows, width), F32),
            ((rows, 1), F32),
            ((rows, width), BF),
            ((4, rows, hidden), BF),
            ((4, rows, hidden), BF),
        ],
        [SMEM] + [VMEM] * 14,
        "forward",
        (place, tokens, *mixed, *outs, *ups, rows_in),
        after,
        lazy={1: rows, **{i: None for i in range(2, 14)}},
        late=(0, 2, 3, 4),
    )


def middle_body(
    io, place, normed1, act, w0, w1, w2, w3, cot, rows_in,
    result_out, res2_out, low_out, d0, d1, d2, d3, sums_out,
):
    down = rows_in[DOWN_BIAS : DOWN_BIAS + 1, :]
    for rel, w in enumerate((w0, w1, w2, w3)):
        io.arrive(2, rel)
        io.arrive(3 + rel)
        down = down + nn(act[rel], w[...])
    io.arrive(1)
    first = normed1[...] * rows_in[GAIN1 : GAIN1 + 1, :] + rows_in[SHIFT1 : SHIFT1 + 1, :]
    gain2 = rows_in[GAIN2 : GAIN2 + 1, :]
    normed, inv = norm_stats(first + down)
    result_out[...] = (normed * gain2 + rows_in[SHIFT2 : SHIFT2 + 1, :]).astype(BF)
    io.leave(0)
    io.arrive(7)
    grad = cot[...].astype(F32)
    res2 = norm_pull(grad, normed, inv, gain2)
    res2_out[...] = res2
    io.leave(1)
    low = res2.astype(BF)
    low_out[...] = low
    io.leave(2)
    sums_out[0:1, :] = col_sum(grad * normed)
    sums_out[1:2, :] = col_sum(grad)
    sums_out[2:3, :] = col_sum(low.astype(F32))
    for rel in (1, 3, 0, 2):
        (d0, d1, d2, d3)[rel][...] = tn(act[rel], low_out[...]).astype(BF)
        io.leave(3 + rel)


def middle(place, normed1, act, downs, cot, rows_in, after=()):
    rows, width = normed1.shape
    hidden = act.shape[2]
    return call(
        middle_body,
        [
            ((rows, width), BF),
            ((rows, width), F32),
            ((rows, width), BF),
        ]
        + [((hidden, width), BF)] * 4
        + [((3, width), F32)],
        [SMEM] + [VMEM] * 8,
        "middle",
        (place, normed1, act, *downs, cot, rows_in),
        after,
        lazy={2: None, 3: None, 4: None, 5: None, 6: None, 1: None, 7: rows},
        late=(0, 1, 2, 3, 4, 5, 6),
    )


def backward_body(
    io, low2, res2, normed1, inv1, slope, w0, w1, w2, w3, u0, u1, u2, u3, o0, o1, o2, o3, rows_in,
    gup_out, res1_out, low_out, gm0, gm1, gm2, gm3, sums_out, ups_out, total,
):
    cols = gm0.shape[1]
    for rel, (w, u) in enumerate(((w0, u0), (w1, u1), (w2, u2), (w3, u3))):

        @pl.loop(0, u.shape[1] // STEP, unroll=3)
        def _(j):
            here = pl.ds(pl.multiple_of(j * STEP, STEP), STEP)
            grad_act = nt(low2[...], w[here, :])
            low = (grad_act * slope[rel, :, here].astype(F32)).astype(BF)
            gup_out[rel, :, here] = low
            ups_out[rel : rel + 1, here] = col_sum(low.astype(F32))
        total[...] = (res2 if rel == 0 else total)[...] + nt(gup_out[rel], u[...])
    grad = total[...]
    res1 = norm_pull(grad, normed1[...], inv1[...], rows_in[GAIN1 : GAIN1 + 1, :])
    res1_out[...] = res1
    low = res1.astype(BF)
    low_out[...] = low
    sums_out[0:1, :] = col_sum(grad * normed1[...])
    sums_out[1:2, :] = col_sum(grad)
    sums_out[2:3, :] = col_sum(low.astype(F32))
    for rel, (gm_out, o) in enumerate(zip((gm0, gm1, gm2, gm3), (o0, o1, o2, o3))):
        gm_out[...] = nt(low, o[0:cols, :]).astype(BF)


def backward(low2, res2, normed1, inv1, slope, downs, ups, outs, rows_in, cols, after=()):
    rows, width = low2.shape
    hidden = slope.shape[2]
    return call(
        backward_body,
        [
            ((4, rows, hidden), BF),
            ((rows, width), F32),
            ((rows, width), BF),
        ]
        + [((rows, cols), BF)] * 4
        + [
            ((3, width), F32),
            ((4, hidden), F32),
        ],
        [VMEM] * 18,
        "backward",
        (low2, res2, normed1, inv1, slope, *downs, *ups, *outs, rows_in),
        after,
        scratch=[pltpu.VMEM((rows, width), F32)],
    )


def up_grads_body(io, low1, gup, *outs):
    for rel in (1, 3, 0, 2):
        outs[rel][...] = tn(low1[:, 0 : outs[rel].shape[0]], gup[rel]).astype(BF)


def up_grads(low1, gup, first, after=()):
    return call(
        up_grads_body,
        [((first, gup.shape[2]), BF)] * 4,
        [VMEM] * 2,
        "up_grads",
        (low1, gup),
        after,
    )


def out_grads_body(io, low1, gup, grad_low, m0, m1, m2, m3, sums1, sums2, ups, *outs):
    width, cols = low1.shape[1], m0.shape[1]
    left = outs[0].shape[0] - cols - PAD
    mixed = (m0, m1, m2, m3)
    for rel in (1, 3, 0, 2):
        out = outs[rel]
        out[0:left, :] = tn(low1[:, width - left :], gup[rel]).astype(BF)
        out[left : left + cols, :] = tn(mixed[rel][...], grad_low[...]).astype(BF)
        rows = jnp.concatenate([sums2[...], sums1[...], ups[rel : rel + 1, :]], 0)
        rows = jnp.concatenate([rows, jnp.zeros((PAD - rows.shape[0], width), F32)], 0)
        out[left + cols :, :] = rows.astype(BF)


def out_grads(low1, gup, grad_low, mixed, sums1, sums2, ups, left, after=()):
    hidden = gup.shape[2]
    cols = mixed[0].shape[1]
    return call(
        out_grads_body,
        [((left + cols + PAD, hidden), BF)] * 4,
        [VMEM] * 10,
        "out_grads",
        (low1, gup, grad_low, *mixed, sums1, sums2, ups),
        after,
    )


def place_rows_body(io, place, p0, p1, p2, p3, out, held, marks):
    quarter = p0.shape[0]
    copies = []
    for rel, p in enumerate((p0, p1, p2, p3)):
        here = pl.ds(pl.multiple_of((place[0] ^ rel) * quarter, quarter), quarter)
        io.arrive(1 + rel)
        held[rel] = p[...].astype(out.dtype)
        copies.append(pltpu.make_async_copy(held.at[rel], out.at[here], marks.at[rel]))
        copies[-1].start()
    for copy in copies:
        copy.wait()


def place_rows(place, parts, dtype, after=()):
    quarter, width = parts[0].shape
    return call(
        place_rows_body,
        [((4 * quarter, width), dtype)],
        [SMEM] + [VMEM] * 4,
        "place_low" if dtype == BF else "place_rows",
        (place, *parts),
        after,
        scratch=[pltpu.VMEM((4, quarter, width), dtype), pltpu.SemaphoreType.DMA((4,))],
        lazy=(1, 2, 3, 4),
        raw=(0,),
    )[0]


def swap(value, axis, bits):
    count = lax.axis_size(axis)
    return lax.ppermute(value, axis, [(i, i ^ bits) for i in range(count)])


def gather_rel(own):
    far = swap(own, "tp", 2)
    return (own, swap(own, "tp", 1), far, swap(far, "tp", 1))


def core_swap(parts):
    return parts[0], swap(parts[1], "tp", 1), parts[2], swap(parts[3], "tp", 1)


def core_sum(keep, got, keep_far, got_far):
    return total(keep, got).astype(BF), total(keep_far, got_far).astype(BF)


def total(keep, got):
    return keep.astype(F32) + got.astype(F32)


def divide(part, level):
    return divide_sum((part,), level)


def divide_sum(parts, level):
    half = parts[0].shape[0] // 2
    first = ((lax.axis_index("seq") >> level) & 1) * half
    send = sum(lax.dynamic_slice_in_dim(p, half - first, half, 0).astype(F32) for p in parts)
    keep = sum(lax.dynamic_slice_in_dim(p, first, half, 0).astype(F32) for p in parts)
    return send.astype(BF), keep


def join(part, other, level):
    upper = ((lax.axis_index("seq") >> level) & 1) != 0
    return jnp.where(
        upper, jnp.concatenate([other, part], 0), jnp.concatenate([part, other], 0)
    )


class Line:
    def __init__(self, first):
        self.last = first

    def take(self, *arrays):
        *arrays, _ = lax.optimization_barrier((*arrays, self.last))
        return arrays if len(arrays) > 1 else arrays[0]

    def put(self, *arrays):
        self.last = arrays[0]
        return arrays if len(arrays) > 1 else arrays[0]


class SeqSum:
    def __init__(self, line, bits):
        self.line, self.bits = line, bits

    def first(self, own, far=None):
        parts = [self.line.take(own)] if far is None else self.line.take(own, far)
        send, self.keep = self.line.put(*divide_sum(parts, self.bits[0]))
        self.got = swap(send, "seq", 1 << self.bits[0])

    def second(self):
        parts = self.line.take(self.keep, self.got)
        send, self.keep = self.line.put(*divide_sum(parts, self.bits[1]))
        self.got = swap(send, "seq", 1 << self.bits[1])

    def third(self):
        part = self.line.put(total(*self.line.take(self.keep, self.got)).astype(BF))
        levels = lax.axis_size("seq").bit_length() - 1
        for k in range(2, levels - 1):
            part = total(part, swap(part, "seq", 1 << k)).astype(BF)
        self.keep, self.got = part, swap(part, "seq", 1 << (levels - 1))

    def fourth(self):
        self.keep = self.line.put(total(*self.line.take(self.keep, self.got)).astype(BF))
        self.got = swap(self.keep, "seq", 1 << self.bits[1])

    def fifth(self):
        self.keep = self.line.put(join(*self.line.take(self.keep, self.got), self.bits[1]))
        self.got = swap(self.keep, "seq", 1 << self.bits[0])

    def sixth(self):
        part, other = self.line.take(self.keep, self.got)
        upper = ((lax.axis_index("seq") >> self.bits[0]) & 1) != 0
        return jnp.where(upper, other, part).astype(F32), jnp.where(upper, part, other).astype(F32)


def on_device(
    tokens, cotangent, lengths, w_qkv, qv_bias, w_out, out_bias, gain_first, shift_first,
    w_up, up_bias, w_down, down_bias, gain_second, shift_second,
):
    rows, width = tokens.shape
    quarter = rows // 4
    cols = w_qkv.shape[2]
    hidden = w_up.shape[1]
    seq_count = lax.axis_size("seq")
    tp_place = lax.axis_index("tp")
    seq_place = lax.axis_index("seq")
    place = jnp.stack([tp_place, seq_place, rows * seq_count]).astype(jnp.int32)
    forwards = [(i, i + 1) for i in range(seq_count - 1)]
    backwards = [(b, a) for a, b in forwards]

    vectors = [out_bias, gain_first, shift_first, down_bias, gain_second, shift_second]
    high, low, bundle, half_d, rows_in = prepare(
        place, tokens, w_out, w_up, w_down, up_bias, vectors
    )
    low, high = lax.ppermute(high, "seq", forwards), lax.ppermute(low, "seq", backwards)
    own_o = bundle[: cols + 16]
    bundle, half_d = swap(bundle, "tp", 2), swap(half_d, "tp", 2)
    wt = jnp.transpose(w_qkv, (0, 2, 1))
    q, k, v, kt, vt, ids_col, ids_row = project(
        place, tokens, wt, qv_bias, lengths.reshape(1, -1), (rows_in,)
    )
    own_o, own_u, own_d, _ = lax.optimization_barrier((own_o, w_up, w_down, q))
    near_o, near_u, near_d = [swap(a, "tp", 1) for a in (own_o, own_u, own_d)]
    p_far, k, v, kt, vt, mixed2, mixed3 = attend_far(
        place, q, k, v, kt, vt, ids_col, ids_row, low, high, wt, qv_bias
    )
    mixed2, mixed3 = swap(mixed2, "tp", 2), swap(mixed3, "tp", 3)
    line = Line(p_far)
    bundle = line.take(bundle)
    far_o, half_u = line.put(bundle[: cols + 16], bundle[cols + 16 :])
    other_u = swap(half_u, "seq", 1)
    last_o = swap(far_o, "tp", 1)
    p_near, mixed0, mixed1 = attend_near(place, q, k, vt, ids_col, ids_row, (line.last,))
    line.put(p_near)
    half_d = line.put(line.take(half_d))
    other_d = swap(half_d, "seq", 1)
    mixed = [mixed0, swap(mixed1, "tp", 1), mixed2, mixed3]
    mixed = line.put(*line.take(*mixed))
    far_u = line.put(join(*line.take(half_u, other_u), 0))
    last_u = swap(far_u, "tp", 1)
    outs, ups = (own_o, near_o, far_o, last_o), (own_u, near_u, far_u, last_u)
    normed1, inv1, low1, act, slope = forward(place, tokens, mixed, outs, ups, rows_in)
    line.put(normed1)
    far_d = line.put(join(*line.take(half_d, other_d), 0))
    downs = (own_d, near_d, far_d, swap(far_d, "tp", 1))
    result, res2, low2, *parts_d, sums2 = middle(
        place, normed1, act, downs, cotangent, rows_in
    )
    act_far, act_near = swap(result, "tp", 2), swap(result, "tp", 1)
    parts_d = core_swap(parts_d)
    gup, res1, grad_low, g0, g1, g2, g3, sums1, up_sums = backward(
        low2, res2, normed1, inv1, slope, downs, ups, outs, rows_in, cols
    )
    g1, g2, g3 = swap(g1, "tp", 1), swap(g2, "tp", 2), swap(g3, "tp", 3)
    own_d, far_d = core_sum(*parts_d)
    left = width - 512
    parts_u = up_grads(low1, gup, width - left, (own_d, far_d, act_far, act_near, g1))
    parts_v = out_grads(
        low1, gup, grad_low, mixed, sums1, sums2, up_sums, left, (parts_u[0],)
    )
    line = Line(parts_v[0])
    sum_d, sum_q, sum_u, sum_v = [
        SeqSum(line, bits) for bits in ((0, 1), (0, 1), (1, 0), (1, 0))
    ]
    firsts = attend_back((0, 1), place, q, k, kt, v, p_near, (g0, g1), (line.last,))
    line.put(firsts[0])
    sum_d.first(own_d, swap(far_d, "tp", 2))
    own_u, far_u = line.put(*core_sum(*line.take(*core_swap(parts_u))))
    *seconds, sum_d.keep = attend_back(
        (2, 3), place, q, k, kt, v, p_far, (g2, g3), (line.last,), (sum_d.keep,)
    )
    line.put(seconds[0])
    low_rim, high_rim = line.put(*rims(tp_place, firsts, seconds))
    from_high = lax.ppermute(low_rim, "seq", backwards)
    from_low = lax.ppermute(high_rim, "seq", forwards)
    own_v, far_v = line.put(*core_sum(*line.take(*core_swap(parts_v))))
    sum_d.second()
    sum_u.first(own_u, swap(far_u, "tp", 2))
    send_q, sum_q.keep, kv, sum_d.keep, sum_u.keep = qkv_grads(
        place, tokens, firsts, seconds, from_low, from_high, (line.last,),
        (sum_d.keep, sum_u.keep),
    )
    sum_q.got = swap(send_q, "seq", 1)
    line.put(send_q)
    sum_d.third()
    sum_u.second()
    act_last = swap(act_far, "tp", 1)
    *parts_i, sum_u.keep, sum_q.keep, own_v = input_back(
        place, firsts[0], seconds[0], kv, wt, (line.last, act_last),
        (sum_u.keep, sum_q.keep, own_v),
    )
    line.put(parts_i[0])
    parts_i = core_swap(parts_i)
    sum_v.first(own_v, swap(far_v, "tp", 2))
    sum_q.second()
    sum_u.third()
    result = place_rows(place, line.take(result, act_near, act_far, act_last), BF)
    line.put(result)
    *parts_i, keep_far, got_far = line.take(*parts_i)
    far_i = swap(line.put(total(keep_far, got_far).astype(BF)), "tp", 2)
    sum_v.second()
    sum_d.fourth()
    sum_q.third()
    sum_u.fourth()
    sum_v.third()
    sum_d.fifth()
    far_i = line.take(far_i)
    part = line.put((total(*parts_i) + far_i.astype(F32) + res1).astype(BF))
    part_far, part_near = swap(part, "tp", 2), swap(part, "tp", 1)
    sum_q.fourth()
    sum_u.fifth()
    sum_v.fourth()
    sum_q.fifth()
    grad_down = line.put(jnp.concatenate(sum_d.sixth(), 0))
    sum_v.fifth()
    part_far = line.put(line.take(part_far))
    part_last = swap(part_far, "tp", 1)
    input_grad = place_rows(place, line.take(part, part_near, part_far, part_last), F32)
    line.put(input_grad)
    lower, upper = sum_q.sixth()
    grad_qkv = line.put(jnp.concatenate([lower, upper[: -PAD]], 0))
    qv_sums = upper[-PAD : 2 - PAD, :cols]
    grad_qkv = jnp.transpose(grad_qkv.reshape(3, cols, width), (0, 2, 1))
    lower, upper = sum_v.sixth()
    grad_up = jnp.concatenate([*sum_u.sixth(), lower, upper[: left - lower.shape[0]]], 0)
    grad_rest = upper[left - lower.shape[0] :]
    grad_out = grad_rest[:cols]
    sums = grad_rest[cols:]
    return (
        result, input_grad, grad_qkv, qv_sums, grad_out, sums[5], sums[3], sums[4],
        grad_up, sums[6], grad_down, sums[2], sums[0], sums[1],
    )


def solution(mesh):
    rep, rows = P(), P("seq", None)
    return jax.shard_map(
        on_device,
        mesh=mesh,
        in_specs=(
            rows, rows, rep, P(None, None, "tp"), P(None, "tp"), P("tp", None), rep, rep, rep,
            P(None, "tp"), P("tp"), P("tp", None), rep, rep, rep,
        ),
        out_specs=(
            rows, rows, P(None, None, "tp"), P(None, "tp"), P("tp", None), rep, rep, rep,
            P(None, "tp"), P("tp"), P("tp", None), rep, rep, rep,
        ),
        check_vma=False,
    )
```

```python
import functools
import types

import jax
import jax.numpy as jnp
from jax import lax
from jax.experimental import pallas as pl
from jax.experimental.pallas import tpu as pltpu
from jax.sharding import PartitionSpec as P

HEAD = 64
MOST = 128
EPS = 1e-12
BF = jnp.bfloat16
F32 = jnp.float32
MIB = 1024 * 1024


def nn(left, right):
    return lax.dot_general(left, right, (((1,), (0,)), ((), ())), preferred_element_type=F32)


def nt(left, right):
    return lax.dot_general(left, right, (((1,), (1,)), ((), ())), preferred_element_type=F32)


def tn(left, right):
    return lax.dot_general(left, right, (((0,), (0,)), ((), ())), preferred_element_type=F32)


VMEM = pl.BlockSpec(memory_space=pltpu.VMEM)
SMEM = pl.BlockSpec(memory_space=pltpu.SMEM)


GRANT = {"place_rows": 16, "place_low": 16, "up_grads": 28, "out_grads": 28, "input_back": 32}
COST = {
    "prepare": 2, "project": 3, "attend_far": 3, "attend_near": 3, "forward": 6, "middle": 5, "backward": 6, "place_rows": 2, "up_grads": 0.5, "out_grads": 0.5, "attend_back": 1, "qkv_grads": 1, "input_back": 3, "place_low": 4,
}
ANY = pl.BlockSpec(memory_space=pl.ANY)


def call(
    body, outs, specs, name, args, after=(), through=(), scratch=(), limit=56, lazy=(), late=(), raw=()
):
    given, extra, made = len(args), len(after) + len(through), len(outs)
    rows_of = dict(lazy) if isinstance(lazy, dict) else {i: None for i in lazy}
    specs = [ANY if i in rows_of else spec for i, spec in enumerate(specs)]

    def split_of(shape):
        return shape[0] if len(shape) > 2 and shape[0] in (2, 4) else 1

    buffers, sems = [], []
    for i, rows in rows_of.items():
        shape = args[i].shape if rows is None else (rows,) + args[i].shape[1:]
        buffers.append(pltpu.VMEM(shape, args[i].dtype))
        sems.append(pltpu.SemaphoreType.DMA((split_of(shape),)))
    for o in late:
        shape, dtype = outs[o]
        buffers.append(pltpu.VMEM(shape, dtype))
        sems.append(pltpu.SemaphoreType.DMA((split_of(shape),)))
    staged = len(buffers)

    def whole(*refs):
        ins, results = list(refs[:given]), list(refs[given + extra : given + extra + made])
        rest = refs[given + extra + made + len(through) :]
        held, marks, rest = rest[:staged], rest[staged : 2 * staged], rest[2 * staged :]
        coming, going, left = {}, {}, []

        def copies(source, target, mark):
            count = split_of(target.shape)
            if count == 1:
                return [pltpu.make_async_copy(source, target, mark.at[0])]
            return [
                pltpu.make_async_copy(source.at[p], target.at[p], mark.at[p]) for p in range(count)
            ]

        for (i, rows), buffer, mark in zip(rows_of.items(), held, marks):
            source = ins[i]
            if rows is not None:
                source = source.at[pl.ds(pl.multiple_of(ins[0][0] * rows, rows), rows)]
            coming[i] = copies(source, buffer, mark)
            ins[i] = buffer
        for o, buffer, mark in zip(late, held[len(rows_of) :], marks[len(rows_of) :]):
            going[o] = copies(buffer, results[o], mark)
            results[o] = buffer
        for group in coming.values():
            for copy in group:
                copy.start()

        def arrive(i, p=0):
            coming[i][p].wait()

        def leave(o, p=0):
            going[o][p].start()
            left.append(going[o][p])

        body(types.SimpleNamespace(arrive=arrive, leave=leave), *ins, *results, *rest)
        for copy in left:
            copy.wait()

    return pl.pallas_call(
        whole,
        out_shape=[jax.ShapeDtypeStruct(shape, dtype) for shape, dtype in outs]
        + [jax.ShapeDtypeStruct(a.shape, a.dtype) for a in through],
        in_specs=list(specs) + [ANY] * extra,
        out_specs=[ANY if o in late or o in raw else VMEM for o in range(made)] + [ANY] * len(through),
        scratch_shapes=buffers + sems + list(scratch),
        name=name,
        input_output_aliases={given + len(after) + n: made + n for n in range(len(through))},
        cost_estimate=pl.CostEstimate(
            flops=int(COST.get(name, 2) * 1_000_000_000), bytes_accessed=0, transcendentals=0
        ),
        compiler_params=pltpu.CompilerParams(vmem_limit_bytes=GRANT.get(name, limit) * MIB),
    )(*args, *after, *through)


def stack_heads(block, heads):
    lane = lax.broadcasted_iota(jnp.int32, block.shape, 1) // HEAD
    zero = jnp.zeros_like(block)
    return jnp.concatenate([jnp.where(lane == h, block, zero) for h in range(heads)], 0)


def pick_heads(stacked, heads):
    size = stacked.shape[1] // heads
    rows = [stacked[h * HEAD : (h + 1) * HEAD, h * size : (h + 1) * size] for h in range(heads)]
    return jnp.concatenate(rows, 0).T


def prepare_body(
    io, place, tokens, w_out, w_up, w_down, up_bias, b0, b1, b2, b3, b4, b5,
    high_out, low_out, own_out, half_down, rows_out, marks,
):
    rows, cols = tokens.shape[0], w_out.shape[0]
    half = half_down.shape[0]
    mine = pl.ds(pl.multiple_of((place[1] & 1) * half, half), half)
    copies = [
        pltpu.make_async_copy(source, target, marks.at[n])
        for n, (source, target) in enumerate(
            (
                (tokens.at[pl.ds(rows - MOST, MOST)], high_out),
                (tokens.at[pl.ds(0, MOST)], low_out),
                (w_out, own_out.at[pl.ds(0, cols)]),
                (w_up.at[mine], own_out.at[pl.ds(cols + 16, half)]),
                (w_down.at[mine], half_down),
            )
        )
    ]
    for copy in copies:
        copy.start()
    rest = up_bias[...].reshape(1, -1)
    pieces = []
    for _ in range(3):
        pieces.append(rest.astype(BF).astype(F32))
        rest = rest - pieces[-1]
    pieces = jnp.concatenate(pieces + [jnp.zeros((13, rest.shape[1]), F32)], 0)
    own_out[cols : cols + 16, :] = pieces.astype(BF)
    rows_out[...] = jnp.zeros_like(rows_out)
    for n, ref in enumerate((b0, b1, b2, b3, b4, b5)):
        rows_out[n : n + 1, :] = ref[...].reshape(1, -1)
    for copy in copies:
        copy.wait()


def prepare(place, tokens, w_out, w_up, w_down, up_bias, vectors):
    width = tokens.shape[1]
    half = (w_up.shape[0] // 2, width)
    return call(
        prepare_body,
        [((MOST, width), BF)] * 2
        + [((w_out.shape[0] + 16 + half[0], width), BF), (half, BF), ((8, width), F32)],
        [SMEM] + [ANY] * 4 + [VMEM] * 7,
        "prepare",
        (place, tokens, w_out, w_up, w_down, up_bias, *vectors),
        scratch=[pltpu.SemaphoreType.DMA((5,))],
    )


def project_block(block, wt, bias, target, k_out, v_out, kt_out, vt_out):
    span = pl.ds(target, block.shape[0])
    keys = nt(block, wt[1])
    k_out[span, :] = keys.astype(BF)
    kt_out[:, span] = keys.T.astype(BF)
    values = nt(block, wt[2]) + bias[1:2, :]
    v_out[span, :] = values.astype(BF)
    vt_out[:, span] = values.T.astype(BF)


def project_body(
    io, place, tokens, wt, bias, lengths, q_out, k_out, v_out, kt_out, vt_out, col_out, row_out
):
    rows = tokens.shape[0]
    ext = col_out.shape[0]
    sents = lengths.shape[1]
    step = 256

    lens = jnp.broadcast_to(lengths[...], (sents, sents))
    down = lax.broadcasted_iota(jnp.int32, (sents, sents), 0)
    across = lax.broadcasted_iota(jnp.int32, (sents, sents), 1)
    ends_col = jnp.sum(jnp.where(across <= down, lens, 0), 1, keepdims=True)
    ends_row = jnp.sum(jnp.where(down == across, ends_col, 0), 0, keepdims=True)
    first = place[1] * rows - MOST

    def sentence(at, ends, axis):
        passed = jnp.sum((ends <= at).astype(jnp.int32), axis, keepdims=True)
        return jnp.where((at < 0) | (at >= place[2]), -1, passed)

    @pl.loop(0, ext // step, unroll=3)
    def _(i):
        base = pl.multiple_of(i * step, step)
        at = first + base
        row_out[:, pl.ds(base, step)] = sentence(
            at + lax.broadcasted_iota(jnp.int32, (1, step), 1), ends_col, 0
        )
        col_out[pl.ds(base, step), :] = sentence(
            at + lax.broadcasted_iota(jnp.int32, (step, 1), 0), ends_row, 1
        )

    io.arrive(1)

    @pl.loop(0, rows // step, unroll=4)
    def _(i):
        first = pl.multiple_of(i * step, step)
        block = tokens[pl.ds(first, step), :]
        q_out[pl.ds(first, step), :] = (nt(block, wt[0]) + bias[0:1, :]).astype(BF)
        target = pl.multiple_of(first + MOST, MOST)
        project_block(block, wt, bias, target, k_out, v_out, kt_out, vt_out)


def project(place, tokens, wt, bias, lengths, after=()):
    rows, cols = tokens.shape[0], wt.shape[1]
    ext = rows + 2 * MOST
    return call(
        project_body,
        [((rows, cols), BF), ((ext, cols), BF), ((ext, cols), BF), ((cols, ext), BF), ((cols, ext), BF)]
        + [((ext, 1), jnp.int32), ((1, ext), jnp.int32)],
        [SMEM] + [VMEM] * 4,
        "project",
        (place, tokens, wt, bias, lengths),
        after,
        lazy=(1,),
    )


def attend_quarters(io, rels, place, q, k, vt, ids_col, ids_row, p_out, mixed_outs):
    rows, cols = q.shape
    heads = cols // HEAD
    scale = jnp.asarray(HEAD**-0.5, BF)
    per = rows // 4 // MOST
    for n, (rel, mixed_out) in enumerate(zip(rels, mixed_outs)):

        @pl.loop(0, per, unroll=4)
        def _(i):
            b = (place[0] ^ rel) * per + i
            first = pl.multiple_of(b * MOST, MOST)
            span = pl.ds(first, 3 * MOST)
            q3 = stack_heads(q[pl.ds(first, MOST), :] * scale, heads)
            scores = nt(k[span, :], q3)
            mine = ids_row[:, pl.ds(pl.multiple_of(first + MOST, MOST), MOST)]
            mask = ids_col[span, :] == mine
            scores = jnp.where(jnp.concatenate([mask] * heads, 1), scores, -1e30)
            raised = jnp.exp(scores - jnp.max(scores, 0, keepdims=True))
            probs = raised * (1.0 / jnp.sum(raised, 0, keepdims=True))
            probs = probs.astype(BF)
            p_out[n, i] = probs
            mixed = pick_heads(nn(vt[:, span], probs), heads)
            mixed_out[pl.ds(pl.multiple_of(i * MOST, MOST), MOST), :] = mixed.astype(BF)

        io.leave(0, n)


def attend_far_body(
    io, place, q, k_in, v_in, kt_in, vt_in, ids_col, ids_row, low, high, wt, bias,
    p_out, k_out, v_out, kt_out, vt_out, m0, m1, marks,
):
    rows = q.shape[0]
    held = (k_out, v_out, kt_out, vt_out)
    copies = [
        pltpu.make_async_copy(source, target, marks.at[n])
        for n, (source, target) in enumerate(zip((k_in, v_in, kt_in, vt_in), held))
    ]
    for copy in copies:
        copy.start()
    for copy in copies:
        copy.wait()
    project_block(low[...], wt, bias, 0, *held)
    project_block(high[...], wt, bias, rows + MOST, *held)
    for o in (1, 2, 3, 4):
        io.leave(o)
    attend_quarters(io, (2, 3), place, q, k_out, vt_out, ids_col, ids_row, p_out, (m0, m1))


def attend_far(place, q, k, v, kt, vt, ids_col, ids_row, low, high, wt, bias, after=()):
    rows, cols = q.shape
    heads = cols // HEAD
    return call(
        attend_far_body,
        [((2, rows // 4 // MOST, 3 * MOST, heads * MOST), BF)]
        + [(a.shape, BF) for a in (k, v, kt, vt)]
        + [((rows // 4, cols), BF)] * 2,
        [SMEM, VMEM] + [ANY] * 4 + [VMEM] * 6,
        "attend_far",
        (place, q, k, v, kt, vt, ids_col, ids_row, low, high, wt, bias),
        after,
        scratch=[pltpu.SemaphoreType.DMA((4,))],
        late=(0, 1, 2, 3, 4),
    )


def attend_near_body(io, place, q, k, vt, ids_col, ids_row, p_out, m0, m1):
    attend_quarters(io, (0, 1), place, q, k, vt, ids_col, ids_row, p_out, (m0, m1))


def attend_near(place, q, k, vt, ids_col, ids_row, after=()):
    rows, cols = q.shape
    heads = cols // HEAD
    return call(
        attend_near_body,
        [((2, rows // 4 // MOST, 3 * MOST, heads * MOST), BF)] + [((rows // 4, cols), BF)] * 2,
        [SMEM] + [VMEM] * 5,
        "attend_near",
        (place, q, k, vt, ids_col, ids_row),
        after,
        late=(0,),
    )


def attend_pull(b, q, k, kt, v, p_low, grad):
    heads = q.shape[1] // HEAD
    scale = jnp.asarray(HEAD**-0.5, BF)
    first = pl.multiple_of(b * MOST, MOST)
    span = pl.ds(first, 3 * MOST)
    g_stack = stack_heads(grad, heads)
    q_stack = stack_heads(q[pl.ds(first, MOST), :] * scale, heads)
    weights = p_low.astype(F32)
    grad_probs = nt(v[span, :], g_stack)
    inner = jnp.sum(weights * grad_probs, 0, keepdims=True)
    grad_scores = (weights * (grad_probs - inner)).astype(BF)
    dq = pick_heads(nn(kt[:, span], grad_scores), heads) * (HEAD**-0.5)
    return dq, nn(grad_scores, q_stack), nn(p_low, g_stack)


def rims(place, first, second):
    flip = (place >> 1) != 0
    ends = []
    for here in (slice(0, MOST), slice(-MOST, None)):
        ends.append([jnp.stack([a[here] for a in side[1:]]) for side in (first, second)])
    low = jnp.where(flip, ends[0][1], ends[0][0]).astype(BF)
    high = jnp.where(flip, ends[1][0], ends[1][1]).astype(BF)
    return low, high


def attend_back_body(rels, io, place, q, k, kt, v, probs, ga, gb, dq_out, dk_out, dv_out):
    quarter = ga.shape[0]
    per = quarter // MOST
    base = ((place[0] ^ rels[0]) >> 1) * (2 * per)
    dk_out[...] = jnp.zeros_like(dk_out)
    dv_out[...] = jnp.zeros_like(dv_out)
    for n, (rel, ref) in enumerate(zip(rels, (ga, gb))):
        io.arrive(5, n)

        @pl.loop(0, per, unroll=4)
        def _(i):
            b = (place[0] ^ rel) * per + i
            rows = pl.ds(pl.multiple_of(i * MOST, MOST), MOST)
            dq, dk, dv = attend_pull(b, q, k, kt, v, probs[n, i], ref[rows, :])
            dq_out[n, rows, :] = dq.astype(BF)
            span = pl.ds(pl.multiple_of((b - base) * MOST, MOST), 3 * MOST)
            dk_out[span, :] += dk
            dv_out[span, :] += dv


def attend_back(rels, place, q, k, kt, v, probs, grads, after=(), through=()):
    rows, cols = q.shape
    half = rows // 2 + 2 * MOST
    return call(
        functools.partial(attend_back_body, rels),
        [((2, rows // 4, cols), BF), ((half, cols), F32), ((half, cols), F32)],
        [SMEM] + [VMEM] * 7,
        "attend_back",
        (place, q, k, kt, v, probs, *grads),
        after,
        through,
        lazy=(5,),
    )


def qkv_grads_body(
    io, place, tokens, dqa, dqb, dka, dkb, dva, dvb, from_low, from_high, send_out, keep_out, kv, sums, dwt
):
    rows = tokens.shape[0]
    cols = kv.shape[2]
    quarter, half = rows // 4, rows // 2
    sums[...] = jnp.zeros_like(sums)
    for side, refs in enumerate(((dka, dva), (dkb, dvb))):
        here = pl.ds(pl.multiple_of(((place[0] >> 1) ^ side) * half, half), half + 2 * MOST)
        for j, ref in enumerate(refs):
            sums[j, here, :] += ref[...]
    for j in range(2):
        sums[j, MOST : 2 * MOST, :] += from_low[j].astype(F32)
        sums[j, rows : rows + MOST, :] += from_high[j].astype(F32)
        kv[j] = sums[j, MOST : rows + MOST, :].astype(BF)
    part = 0
    for rel, d in enumerate((dqa.at[0], dqa.at[1], dqb.at[0], dqb.at[1])):
        here = pl.ds(pl.multiple_of((place[0] ^ rel) * quarter, quarter), quarter)
        part = part + tn(d[...], tokens[here, :])
    dwt[0:cols, :] = part
    dwt[cols : 2 * cols, :] = tn(kv[0], tokens[...])
    dwt[2 * cols : 3 * cols, :] = tn(kv[1], tokens[...])
    dwt[3 * cols :, :] = jnp.zeros_like(dwt[3 * cols :, :])
    totals = [col_sum(d[n].astype(F32)) for d in (dqa, dqb) for n in range(2)]
    dwt[3 * cols : 3 * cols + 1, 0:cols] = sum(totals)
    dwt[3 * cols + 1 : 3 * cols + 2, 0:cols] = col_sum(kv[1].astype(F32))
    size = keep_out.shape[0]
    bit = place[1] & 1
    keep_out[...] = dwt[pl.ds(pl.multiple_of(bit * size, size), size), :]
    send_out[...] = dwt[pl.ds(pl.multiple_of((1 - bit) * size, size), size), :].astype(BF)


def qkv_grads(place, tokens, firsts, seconds, from_low, from_high, after=(), through=()):
    (rows, width), cols = tokens.shape, from_low.shape[2]
    pairs = [a for pair in zip(firsts, seconds) for a in pair]
    size = (3 * cols + PAD) // 2
    return call(
        qkv_grads_body,
        [((size, width), BF), ((size, width), F32), ((2, rows, cols), BF)],
        [SMEM] + [VMEM] * 9,
        "qkv_grads",
        (place, tokens, *pairs, from_low, from_high),
        after,
        through,
        scratch=[
            pltpu.VMEM((2, rows + 2 * MOST, cols), F32),
            pltpu.VMEM((3 * cols + PAD, width), F32),
        ],
    )


def input_back_body(io, place, dqa, dqb, kv, wt, *outs):
    quarter = kv.shape[1] // 4
    dq = [dqa.at[0], dqa.at[1], dqb.at[0], dqb.at[1]]
    for rel in (1, 3, 0, 2):
        here = pl.ds(pl.multiple_of((place[0] ^ rel) * quarter, quarter), quarter)
        part = nn(dq[rel][...], wt[0]) + nn(kv[0, here, :], wt[1]) + nn(kv[1, here, :], wt[2])
        outs[rel][...] = part.astype(outs[rel].dtype)


def input_back(place, dqa, dqb, kv, wt, after=(), through=()):
    rows, width = kv.shape[1], wt.shape[2]
    return call(
        input_back_body,
        [((rows // 4, width), BF if rel % 2 else F32) for rel in range(4)],
        [SMEM] + [VMEM] * 4,
        "input_back",
        (place, dqa, dqb, kv, wt),
        after,
        through,
    )


def gelu_parts(pre):
    size = jnp.abs(pre) * (0.5**0.5)
    bell = jnp.exp(-size * size)
    t = 1.0 / (1.0 + 0.3275911 * size)
    poly = 1.061405429
    for c in (-1.453152027, 1.421413741, -0.284496736, 0.254829592):
        poly = poly * t + c
    tail = 0.5 * poly * t * bell
    cdf = jnp.where(pre >= 0, 1.0 - tail, tail)
    return pre * cdf, cdf + pre * bell * 0.3989422804014327


def norm_stats(resid):
    centred = resid - jnp.mean(resid, -1, keepdims=True)
    inv = lax.rsqrt(jnp.mean(centred * centred, -1, keepdims=True) + EPS)
    return centred * inv, inv


def norm_pull(grad, normed, inv, gain):
    scaled = grad * gain
    return inv * (
        scaled
        - jnp.mean(scaled, -1, keepdims=True)
        - normed * jnp.mean(scaled * normed, -1, keepdims=True)
    )


def col_sum(values):
    return jnp.sum(values, 0, keepdims=True)


STEP = 256
PAD = 64
OUT_BIAS, GAIN1, SHIFT1, DOWN_BIAS, GAIN2, SHIFT2 = range(6)


def forward_body(
    io, place, tokens, m0, m1, m2, m3, o0, o1, o2, o3, u0, u1, u2, u3, rows_in,
    normed_out, inv_out, low_out, act_out, slope_out,
):
    cols = m0.shape[1]
    attn = rows_in[OUT_BIAS : OUT_BIAS + 1, :]
    for rel, (m, o) in enumerate(((m0, o0), (m1, o1), (m2, o2), (m3, o3))):
        io.arrive(2 + rel)
        io.arrive(6 + rel)
        attn = attn + nn(m[...], o[0:cols, :])
    io.arrive(1)
    normed, inv = norm_stats(tokens[...].astype(F32) + attn)
    normed_out[...] = normed
    inv_out[...] = inv
    low_out[...] = (normed * rows_in[GAIN1 : GAIN1 + 1, :] + rows_in[SHIFT1 : SHIFT1 + 1, :]).astype(BF)
    io.leave(0)
    io.leave(2)
    for rel, (u, o) in enumerate(((u0, o0), (u1, o1), (u2, o2), (u3, o3))):
        io.arrive(10 + rel)

        @pl.loop(0, u.shape[1] // STEP, unroll=3)
        def _(j):
            here = pl.ds(pl.multiple_of(j * STEP, STEP), STEP)
            bias = col_sum(o[cols : cols + 16, here].astype(F32))
            act, slope = gelu_parts(nn(low_out[...], u[:, here]) + bias)
            act_out[rel, :, here] = act.astype(BF)
            slope_out[rel, :, here] = slope.astype(BF)

        io.leave(3, rel)
        io.leave(4, rel)


def forward(place, tokens, mixed, outs, ups, rows_in, after=()):
    rows, width = tokens.shape[0] // 4, tokens.shape[1]
    hidden = ups[0].shape[1]
    return call(
        forward_body,
        [
            ((rows, width), F32),
            ((rows, 1), F32),
            ((rows, width), BF),
            ((4, rows, hidden), BF),
            ((4, rows, hidden), BF),
        ],
        [SMEM] + [VMEM] * 14,
        "forward",
        (place, tokens, *mixed, *outs, *ups, rows_in),
        after,
        lazy={1: rows, **{i: None for i in range(2, 14)}},
        late=(0, 2, 3, 4),
    )


def middle_body(
    io, place, normed1, act, w0, w1, w2, w3, cot, rows_in,
    result_out, res2_out, low_out, d0, d1, d2, d3, sums_out,
):
    down = rows_in[DOWN_BIAS : DOWN_BIAS + 1, :]
    for rel, w in enumerate((w0, w1, w2, w3)):
        io.arrive(2, rel)
        io.arrive(3 + rel)
        down = down + nn(act[rel], w[...])
    io.arrive(1)
    first = normed1[...] * rows_in[GAIN1 : GAIN1 + 1, :] + rows_in[SHIFT1 : SHIFT1 + 1, :]
    gain2 = rows_in[GAIN2 : GAIN2 + 1, :]
    normed, inv = norm_stats(first + down)
    result_out[...] = (normed * gain2 + rows_in[SHIFT2 : SHIFT2 + 1, :]).astype(BF)
    io.leave(0)
    io.arrive(7)
    grad = cot[...].astype(F32)
    res2 = norm_pull(grad, normed, inv, gain2)
    res2_out[...] = res2
    io.leave(1)
    low = res2.astype(BF)
    low_out[...] = low
    io.leave(2)
    sums_out[0:1, :] = col_sum(grad * normed)
    sums_out[1:2, :] = col_sum(grad)
    sums_out[2:3, :] = col_sum(low.astype(F32))
    for rel in (1, 3, 0, 2):
        (d0, d1, d2, d3)[rel][...] = tn(act[rel], low_out[...]).astype(BF)
        io.leave(3 + rel)


def middle(place, normed1, act, downs, cot, rows_in, after=()):
    rows, width = normed1.shape
    hidden = act.shape[2]
    return call(
        middle_body,
        [
            ((rows, width), BF),
            ((rows, width), F32),
            ((rows, width), BF),
        ]
        + [((hidden, width), BF)] * 4
        + [((3, width), F32)],
        [SMEM] + [VMEM] * 8,
        "middle",
        (place, normed1, act, *downs, cot, rows_in),
        after,
        lazy={2: None, 3: None, 4: None, 5: None, 6: None, 1: None, 7: rows},
        late=(0, 1, 2, 3, 4, 5, 6),
    )


def backward_body(
    io, low2, res2, normed1, inv1, slope, w0, w1, w2, w3, u0, u1, u2, u3, o0, o1, o2, o3, rows_in,
    gup_out, res1_out, low_out, gm0, gm1, gm2, gm3, sums_out, ups_out, total,
):
    cols = gm0.shape[1]
    for rel, (w, u) in enumerate(((w0, u0), (w1, u1), (w2, u2), (w3, u3))):

        @pl.loop(0, u.shape[1] // STEP, unroll=3)
        def _(j):
            here = pl.ds(pl.multiple_of(j * STEP, STEP), STEP)
            grad_act = nt(low2[...], w[here, :])
            low = (grad_act * slope[rel, :, here].astype(F32)).astype(BF)
            gup_out[rel, :, here] = low
            ups_out[rel : rel + 1, here] = col_sum(low.astype(F32))
        total[...] = (res2 if rel == 0 else total)[...] + nt(gup_out[rel], u[...])
    grad = total[...]
    res1 = norm_pull(grad, normed1[...], inv1[...], rows_in[GAIN1 : GAIN1 + 1, :])
    res1_out[...] = res1
    low = res1.astype(BF)
    low_out[...] = low
    sums_out[0:1, :] = col_sum(grad * normed1[...])
    sums_out[1:2, :] = col_sum(grad)
    sums_out[2:3, :] = col_sum(low.astype(F32))
    for rel, (gm_out, o) in enumerate(zip((gm0, gm1, gm2, gm3), (o0, o1, o2, o3))):
        gm_out[...] = nt(low, o[0:cols, :]).astype(BF)


def backward(low2, res2, normed1, inv1, slope, downs, ups, outs, rows_in, cols, after=()):
    rows, width = low2.shape
    hidden = slope.shape[2]
    return call(
        backward_body,
        [
            ((4, rows, hidden), BF),
            ((rows, width), F32),
            ((rows, width), BF),
        ]
        + [((rows, cols), BF)] * 4
        + [
            ((3, width), F32),
            ((4, hidden), F32),
        ],
        [VMEM] * 18,
        "backward",
        (low2, res2, normed1, inv1, slope, *downs, *ups, *outs, rows_in),
        after,
        scratch=[pltpu.VMEM((rows, width), F32)],
    )


def up_grads_body(io, low1, gup, *outs):
    for rel in (1, 3, 0, 2):
        outs[rel][...] = tn(low1[:, 0 : outs[rel].shape[0]], gup[rel]).astype(BF)


def up_grads(low1, gup, first, after=()):
    return call(
        up_grads_body,
        [((first, gup.shape[2]), BF)] * 4,
        [VMEM] * 2,
        "up_grads",
        (low1, gup),
        after,
    )


def out_grads_body(io, low1, gup, grad_low, m0, m1, m2, m3, sums1, sums2, ups, *outs):
    width, cols = low1.shape[1], m0.shape[1]
    left = outs[0].shape[0] - cols - PAD
    mixed = (m0, m1, m2, m3)
    for rel in (1, 3, 0, 2):
        out = outs[rel]
        out[0:left, :] = tn(low1[:, width - left :], gup[rel]).astype(BF)
        out[left : left + cols, :] = tn(mixed[rel][...], grad_low[...]).astype(BF)
        rows = jnp.concatenate([sums2[...], sums1[...], ups[rel : rel + 1, :]], 0)
        rows = jnp.concatenate([rows, jnp.zeros((PAD - rows.shape[0], width), F32)], 0)
        out[left + cols :, :] = rows.astype(BF)


def out_grads(low1, gup, grad_low, mixed, sums1, sums2, ups, left, after=()):
    hidden = gup.shape[2]
    cols = mixed[0].shape[1]
    return call(
        out_grads_body,
        [((left + cols + PAD, hidden), BF)] * 4,
        [VMEM] * 10,
        "out_grads",
        (low1, gup, grad_low, *mixed, sums1, sums2, ups),
        after,
    )


def place_rows_body(io, place, p0, p1, p2, p3, out, held, marks):
    quarter = p0.shape[0]
    copies = []
    for rel, p in enumerate((p0, p1, p2, p3)):
        here = pl.ds(pl.multiple_of((place[0] ^ rel) * quarter, quarter), quarter)
        io.arrive(1 + rel)
        held[rel] = p[...].astype(out.dtype)
        copies.append(pltpu.make_async_copy(held.at[rel], out.at[here], marks.at[rel]))
        copies[-1].start()
    for copy in copies:
        copy.wait()


def place_rows(place, parts, dtype, after=()):
    quarter, width = parts[0].shape
    return call(
        place_rows_body,
        [((4 * quarter, width), dtype)],
        [SMEM] + [VMEM] * 4,
        "place_low" if dtype == BF else "place_rows",
        (place, *parts),
        after,
        scratch=[pltpu.VMEM((4, quarter, width), dtype), pltpu.SemaphoreType.DMA((4,))],
        lazy=(1, 2, 3, 4),
        raw=(0,),
    )[0]


def swap(value, axis, bits):
    count = lax.axis_size(axis)
    return lax.ppermute(value, axis, [(i, i ^ bits) for i in range(count)])


def gather_rel(own):
    far = swap(own, "tp", 2)
    return (own, swap(own, "tp", 1), far, swap(far, "tp", 1))


def core_swap(parts):
    return parts[0], swap(parts[1], "tp", 1), parts[2], swap(parts[3], "tp", 1)


def core_sum(keep, got, keep_far, got_far):
    return total(keep, got).astype(BF), total(keep_far, got_far).astype(BF)


def total(keep, got):
    return keep.astype(F32) + got.astype(F32)


def divide(part, level):
    return divide_sum((part,), level)


def divide_sum(parts, level):
    half = parts[0].shape[0] // 2
    first = ((lax.axis_index("seq") >> level) & 1) * half
    send = sum(lax.dynamic_slice_in_dim(p, half - first, half, 0).astype(F32) for p in parts)
    keep = sum(lax.dynamic_slice_in_dim(p, first, half, 0).astype(F32) for p in parts)
    return send.astype(BF), keep


def join(part, other, level):
    upper = ((lax.axis_index("seq") >> level) & 1) != 0
    return jnp.where(
        upper, jnp.concatenate([other, part], 0), jnp.concatenate([part, other], 0)
    )


class Line:
    def __init__(self, first):
        self.last = first

    def take(self, *arrays):
        *arrays, _ = lax.optimization_barrier((*arrays, self.last))
        return arrays if len(arrays) > 1 else arrays[0]

    def put(self, *arrays):
        self.last = arrays[0]
        return arrays if len(arrays) > 1 else arrays[0]


class SeqSum:
    def __init__(self, line, bits):
        self.line, self.bits = line, bits

    def first(self, own, far=None):
        parts = [self.line.take(own)] if far is None else self.line.take(own, far)
        send, self.keep = self.line.put(*divide_sum(parts, self.bits[0]))
        self.got = swap(send, "seq", 1 << self.bits[0])

    def second(self):
        parts = self.line.take(self.keep, self.got)
        send, self.keep = self.line.put(*divide_sum(parts, self.bits[1]))
        self.got = swap(send, "seq", 1 << self.bits[1])

    def third(self):
        part = self.line.put(total(*self.line.take(self.keep, self.got)).astype(BF))
        levels = lax.axis_size("seq").bit_length() - 1
        for k in range(2, levels - 1):
            part = total(part, swap(part, "seq", 1 << k)).astype(BF)
        self.keep, self.got = part, swap(part, "seq", 1 << (levels - 1))

    def fourth(self):
        self.keep = self.line.put(total(*self.line.take(self.keep, self.got)).astype(BF))
        self.got = swap(self.keep, "seq", 1 << self.bits[1])

    def fifth(self):
        self.keep = self.line.put(join(*self.line.take(self.keep, self.got), self.bits[1]))
        self.got = swap(self.keep, "seq", 1 << self.bits[0])

    def sixth(self):
        part, other = self.line.take(self.keep, self.got)
        upper = ((lax.axis_index("seq") >> self.bits[0]) & 1) != 0
        return jnp.where(upper, other, part).astype(F32), jnp.where(upper, part, other).astype(F32)


def on_device(
    tokens, cotangent, lengths, w_qkv, qv_bias, w_out, out_bias, gain_first, shift_first,
    w_up, up_bias, w_down, down_bias, gain_second, shift_second,
):
    rows, width = tokens.shape
    quarter = rows // 4
    cols = w_qkv.shape[2]
    hidden = w_up.shape[1]
    seq_count = lax.axis_size("seq")
    tp_place = lax.axis_index("tp")
    seq_place = lax.axis_index("seq")
    place = jnp.stack([tp_place, seq_place, rows * seq_count]).astype(jnp.int32)
    forwards = [(i, i + 1) for i in range(seq_count - 1)]
    backwards = [(b, a) for a, b in forwards]

    vectors = [out_bias, gain_first, shift_first, down_bias, gain_second, shift_second]
    high, low, bundle, half_d, rows_in = prepare(
        place, tokens, w_out, w_up, w_down, up_bias, vectors
    )
    low, high = lax.ppermute(high, "seq", forwards), lax.ppermute(low, "seq", backwards)
    own_o = bundle[: cols + 16]
    bundle, half_d = swap(bundle, "tp", 2), swap(half_d, "tp", 2)
    wt = jnp.transpose(w_qkv, (0, 2, 1))
    q, k, v, kt, vt, ids_col, ids_row = project(
        place, tokens, wt, qv_bias, lengths.reshape(1, -1), (rows_in,)
    )
    own_o, own_u, own_d, _ = lax.optimization_barrier((own_o, w_up, w_down, q))
    near_o, near_u, near_d = [swap(a, "tp", 1) for a in (own_o, own_u, own_d)]
    p_far, k, v, kt, vt, mixed2, mixed3 = attend_far(
        place, q, k, v, kt, vt, ids_col, ids_row, low, high, wt, qv_bias
    )
    mixed2, mixed3 = swap(mixed2, "tp", 2), swap(mixed3, "tp", 3)
    line = Line(p_far)
    bundle = line.take(bundle)
    far_o, half_u = line.put(bundle[: cols + 16], bundle[cols + 16 :])
    other_u = swap(half_u, "seq", 1)
    last_o = swap(far_o, "tp", 1)
    p_near, mixed0, mixed1 = attend_near(place, q, k, vt, ids_col, ids_row, (line.last,))
    line.put(p_near)
    half_d = line.put(line.take(half_d))
    other_d = swap(half_d, "seq", 1)
    mixed = [mixed0, swap(mixed1, "tp", 1), mixed2, mixed3]
    mixed = line.put(*line.take(*mixed))
    far_u = line.put(join(*line.take(half_u, other_u), 0))
    last_u = swap(far_u, "tp", 1)
    outs, ups = (own_o, near_o, far_o, last_o), (own_u, near_u, far_u, last_u)
    normed1, inv1, low1, act, slope = forward(place, tokens, mixed, outs, ups, rows_in)
    line.put(normed1)
    far_d = line.put(join(*line.take(half_d, other_d), 0))
    downs = (own_d, near_d, far_d, swap(far_d, "tp", 1))
    result, res2, low2, *parts_d, sums2 = middle(
        place, normed1, act, downs, cotangent, rows_in
    )
    act_far, act_near = swap(result, "tp", 2), swap(result, "tp", 1)
    parts_d = core_swap(parts_d)
    gup, res1, grad_low, g0, g1, g2, g3, sums1, up_sums = backward(
        low2, res2, normed1, inv1, slope, downs, ups, outs, rows_in, cols
    )
    g1, g2, g3 = swap(g1, "tp", 1), swap(g2, "tp", 2), swap(g3, "tp", 3)
    own_d, far_d = core_sum(*parts_d)
    left = width - 512
    parts_u = up_grads(low1, gup, width - left, (own_d, far_d, act_far, act_near, g1))
    parts_v = out_grads(
        low1, gup, grad_low, mixed, sums1, sums2, up_sums, left, (parts_u[0],)
    )
    line = Line(parts_v[0])
    sum_d, sum_q, sum_u, sum_v = [
        SeqSum(line, bits) for bits in ((0, 1), (0, 1), (1, 0), (1, 0))
    ]
    firsts = attend_back((0, 1), place, q, k, kt, v, p_near, (g0, g1), (line.last,))
    line.put(firsts[0])
    sum_d.first(own_d, swap(far_d, "tp", 2))
    own_u, far_u = line.put(*core_sum(*line.take(*core_swap(parts_u))))
    *seconds, sum_d.keep = attend_back(
        (2, 3), place, q, k, kt, v, p_far, (g2, g3), (line.last,), (sum_d.keep,)
    )
    line.put(seconds[0])
    low_rim, high_rim = line.put(*rims(tp_place, firsts, seconds))
    from_high = lax.ppermute(low_rim, "seq", backwards)
    from_low = lax.ppermute(high_rim, "seq", forwards)
    own_v, far_v = line.put(*core_sum(*line.take(*core_swap(parts_v))))
    sum_d.second()
    sum_u.first(own_u, swap(far_u, "tp", 2))
    send_q, sum_q.keep, kv, sum_d.keep, sum_u.keep = qkv_grads(
        place, tokens, firsts, seconds, from_low, from_high, (line.last,),
        (sum_d.keep, sum_u.keep),
    )
    sum_q.got = swap(send_q, "seq", 1)
    line.put(send_q)
    sum_d.third()
    sum_u.second()
    act_last = swap(act_far, "tp", 1)
    *parts_i, sum_u.keep, sum_q.keep, own_v = input_back(
        place, firsts[0], seconds[0], kv, wt, (line.last, act_last),
        (sum_u.keep, sum_q.keep, own_v),
    )
    line.put(parts_i[0])
    parts_i = core_swap(parts_i)
    sum_v.first(own_v, swap(far_v, "tp", 2))
    sum_q.second()
    sum_u.third()
    result = place_rows(place, line.take(result, act_near, act_far, act_last), BF)
    line.put(result)
    *parts_i, keep_far, got_far = line.take(*parts_i)
    far_i = swap(line.put(total(keep_far, got_far).astype(BF)), "tp", 2)
    sum_v.second()
    sum_d.fourth()
    sum_q.third()
    sum_u.fourth()
    sum_v.third()
    sum_d.fifth()
    far_i = line.take(far_i)
    part = line.put((total(*parts_i) + far_i.astype(F32) + res1).astype(BF))
    part_far, part_near = swap(part, "tp", 2), swap(part, "tp", 1)
    sum_q.fourth()
    sum_u.fifth()
    sum_v.fourth()
    sum_q.fifth()
    grad_down = line.put(jnp.concatenate(sum_d.sixth(), 0))
    sum_v.fifth()
    part_far = line.put(line.take(part_far))
    part_last = swap(part_far, "tp", 1)
    input_grad = place_rows(place, line.take(part, part_near, part_far, part_last), F32)
    line.put(input_grad)
    lower, upper = sum_q.sixth()
    grad_qkv = line.put(jnp.concatenate([lower, upper[: -PAD]], 0))
    qv_sums = upper[-PAD : 2 - PAD, :cols]
    grad_qkv = jnp.transpose(grad_qkv.reshape(3, cols, width), (0, 2, 1))
    lower, upper = sum_v.sixth()
    grad_up = jnp.concatenate([*sum_u.sixth(), lower, upper[: left - lower.shape[0]]], 0)
    grad_rest = upper[left - lower.shape[0] :]
    grad_out = grad_rest[:cols]
    sums = grad_rest[cols:]
    return (
        result, input_grad, grad_qkv, qv_sums, grad_out, sums[5], sums[3], sums[4],
        grad_up, sums[6], grad_down, sums[2], sums[0], sums[1],
    )


def solution(mesh):
    rep, rows = P(), P("seq", None)
    return jax.shard_map(
        on_device,
        mesh=mesh,
        in_specs=(
            rows, rows, rep, P(None, None, "tp"), P(None, "tp"), P("tp", None), rep, rep, rep,
            P(None, "tp"), P("tp"), P("tp", None), rep, rep, rep,
        ),
        out_specs=(
            rows, rows, P(None, None, "tp"), P(None, "tp"), P("tp", None), rep, rep, rep,
            P(None, "tp"), P("tp"), P("tp", None), rep, rep, rep,
        ),
        check_vma=False,
    )
```
